512 devices in a mesh: tile: 32 (over z, x_lo), mode: 16 (over y, x_hi, core).
Axes of the slice: x: 4 (x_hi: 2, x_lo: 2; x = x_hi * 2 + x_lo), y: 4, z: 16, core: 2. Of those that a mesh axis runs over, the one named last changes fastest.
Arguments:
- charges: bfloat16 [512, 2, 32768], P('mode', None, 'tile'), may hold values from -6 to 6
- proxy: bfloat16 [512, 256, 128], P('mode'), may hold values from -0.5 to 0.5
- tile_boxes: int32 [4096, 4], P('tile'), may hold values from 0 to 1023, as said below
- box_skel: int32 [1024, 32], replicated, may hold values from 0 to 32767, as said below
Outputs:
- potential: bfloat16 [256, 4096, 1024], P('mode', 'tile')
The draws below stay inside these ranges and needn't reach their ends.
Inputs may be any that keep to these rules, and one draw needn't show every extreme that they name: `tile_boxes`: every box named for a tile of rows [i * 128, (i + 1) * 128) belongs to an index within 1 of i, box b belonging to index b // 32. `box_skel`: the indices of one box are distinct and lie in [o * 1024, (o + 1) * 1024) with o = b // 32; no two boxes share an index.
All inputs are finite; a program needn't handle non-finite values.
Results may differ from the reference program's by a relative error of at most 0.0055.
Values may be sent and summed in bfloat16 or wider, within the bound.
No kernel may reach another device: no remote copies, remote signals or barrier semaphores. Data moves between devices by JAX's collectives and lax.ppermute only.
A program may use at most 64 MiB of HBM per device.

```python
import math
import jax
import jax.numpy as jnp
from jax import lax

MODES = 512
TPT = 256
S = 32
L = 4
TILES_DEV = 128
BOXES_DEV = 32
ANGLES = 1024
SKEL_DEV = 1024
TILES = 4096
BOXES = 1024
SKEL = 32768


def draw_tile_boxes(key, part):
    key = jax.random.fold_in(key, 11)
    key_offset, key_local = jax.random.split(key)
    owners = TILES // TILES_DEV
    rows = jnp.arange(TILES, dtype=jnp.int32)
    device = rows // TILES_DEV
    offset = jax.random.randint(key_offset, (TILES, L), -1, 2, dtype=jnp.int32)
    owner = jnp.clip(device[:, None] + offset, 0, owners - 1)
    local = jax.random.randint(key_local, (TILES, L), 0, BOXES_DEV, dtype=jnp.int32)
    boxes = owner * BOXES_DEV + local
    boxes = boxes.at[0, 0].set(0)
    boxes = boxes.at[TILES - 1, L - 1].set(BOXES - 1)
    return boxes.astype(jnp.int32)


def draw_box_skel(key, part):
    key = jax.random.fold_in(key, 23)
    owners = BOXES // BOXES_DEV

    def one_owner(owner):
        order = jax.random.permutation(jax.random.fold_in(key, owner), SKEL_DEV).astype(jnp.int32)
        return owner * SKEL_DEV + order
    table = jax.vmap(one_owner)(jnp.arange(owners, dtype=jnp.int32))
    return table.reshape(BOXES, S).astype(jnp.int32)


def shard_levels(key, dims, pieces, least, high):
    def one(position, blocks):
        heights = jax.random.uniform(jax.random.fold_in(jax.random.fold_in(key, 6), position), (blocks,), jnp.float32, least / len(pieces), high / len(pieces))
        return jnp.repeat(jnp.exp(heights), dims[position] // blocks).reshape((-1,) + (1,) * (len(dims) - position - 1))

    factor_of = one(*pieces[0])
    for cut in pieces[1:]:
        factor_of = factor_of * one(*cut)
    return factor_of


def normal_values(key, dims, deviation, most, cuts=(), kind=jnp.bfloat16):
    values = jax.random.normal(key, dims, jnp.float32) * deviation
    if len(cuts) > 0:
        values = shard_levels(key, dims, cuts, -0.22, 0.18) * values
    return jnp.clip(values, min=-most, max=most).astype(kind)


def setup_inputs(seed: int = 0) -> dict:
    streams_of = jax.random.split(jax.random.key(seed), 5)
    return {
        "charges": normal_values(streams_of[0], (MODES, 2, SKEL), 1.0, 6.0, ((0, 16), (2, 32))),
        "proxy": normal_values(streams_of[1], (MODES, TPT, L * S), (L * S) ** -0.5, 0.5, ((0, 16),)),
        "tile_boxes": draw_tile_boxes(jax.random.fold_in(streams_of[4], 71), 0),
        "box_skel": draw_box_skel(jax.random.fold_in(streams_of[4], 71), 0),
    }


def synthesis_table(modes):
    angles = 2 * modes
    order = jnp.arange(modes, dtype=jnp.int32)
    angle_ids = jnp.arange(angles, dtype=jnp.int32)
    phase = (order[:, None] * angle_ids[None, :] % angles).astype(jnp.float32) * (2.0 * math.pi / angles)
    weight = jnp.where(order == 0, 1.0, 2.0).astype(jnp.float32) / math.sqrt(2.0 * modes)
    table = jnp.stack([weight[:, None] * jnp.cos(phase), -weight[:, None] * jnp.sin(phase)], axis=1)
    return table.reshape(2 * modes, angles).astype(jnp.bfloat16)

def reference(charges, proxy, tile_boxes, box_skel):
    table = synthesis_table(MODES)
    listed = jnp.take(box_skel, tile_boxes.reshape(-1), axis=0).reshape(TILES // TILES_DEV, TILES_DEV, L * S)
    proxy_wide = proxy.astype(jnp.float32)

    def one_block(block_ids):
        picked = jnp.take(charges, block_ids.reshape(-1), axis=2).astype(jnp.float32)
        picked = picked.reshape(MODES, 2, TILES_DEV, L * S)
        field = jnp.einsum('mctk,mpk->mcpt', picked, proxy_wide).astype(jnp.bfloat16)
        flat = field.reshape(2 * MODES, TPT * TILES_DEV)
        result = jnp.dot(flat.T, table, preferred_element_type=jnp.float32)
        return result.reshape(TPT, TILES_DEV, ANGLES).astype(jnp.bfloat16)
    blocks = lax.map(one_block, listed)
    return jnp.transpose(blocks, (1, 0, 2, 3)).reshape(TPT, TILES, ANGLES)
```

```python
import math

import jax
import jax.numpy as jnp
from jax import lax
from jax.experimental import pallas as pl
from jax.experimental.pallas import tpu as pltpu
from jax.sharding import PartitionSpec as P

BF16 = jnp.bfloat16
F32 = jnp.float32
LANES = 128
SUBS = 8


def half_table(modes):
    angles = 2 * modes
    row = lax.broadcasted_iota(jnp.int32, (2 * modes, modes), 0)
    angle = lax.broadcasted_iota(jnp.int32, (2 * modes, modes), 1)
    parity = row // modes
    rest = row % modes
    order = (rest // 2) * 2 + parity
    phase = (order * angle % angles).astype(F32) * (2.0 * math.pi / angles)
    weight = jnp.where(order == 0, 1.0, 2.0).astype(F32) / math.sqrt(2.0 * modes)
    return jnp.where(rest % 2 == 0, weight * jnp.cos(phase), -weight * jnp.sin(phase)).astype(BF16)


def order_kernel(width, tile_ref, charges_ref, skel_ref, out_ref, hot, rows):
    slots, boxes = skel_ref.shape[0], slots_boxes(width, skel_ref.shape[0])
    tile = tile_ref[0]
    per_block = LANES // boxes
    groups = slots // SUBS
    lane = lax.broadcasted_iota(jnp.int32, (SUBS, LANES), 1)
    index = jnp.zeros((SUBS, LANES), jnp.int32)
    for u in range(groups):
        part = skel_ref[u * SUBS : (u + 1) * SUBS, :]
        shift = lax.rem(u * boxes - lax.rem(tile, per_block) * boxes + LANES, LANES)
        moved = pltpu.roll(part, shift, 1)
        index = jnp.where(lane // boxes == u, moved, index)
    index = index - tile * width
    spot = lax.broadcasted_iota(jnp.int32, (width, LANES), 0)
    for q in range(SUBS):
        hot[:, q * LANES : (q + 1) * LANES] = jnp.where(spot == index[q : q + 1, :], 1.0, 0.0).astype(BF16)
    count = charges_ref.shape[0]
    moved = jnp.dot(charges_ref[...], hot[...], preferred_element_type=F32)
    for q in range(SUBS):
        rows[pl.ds(q, count, stride=SUBS), :] = moved[:, q * LANES : (q + 1) * LANES]
    out_ref[...] = rows[...].astype(BF16)


def slots_boxes(width, slots):
    return width // slots


def box_order(charges, skel_t, tile):
    count, width = charges.shape
    slots = skel_t.shape[0]
    per_block = LANES // slots_boxes(width, slots)
    rows = count * SUBS

    def body(tile_ref, charges_ref, skel_ref, out_ref, hot, scratch):
        order_kernel(width, tile_ref, charges_ref, skel_ref, out_ref, hot, scratch)

    return pl.pallas_call(
        body,
        out_shape=jax.ShapeDtypeStruct((rows, LANES), BF16),
        grid_spec=pltpu.PrefetchScalarGridSpec(
            num_scalar_prefetch=1,
            grid=(1,),
            in_specs=[
                pl.BlockSpec((count, width), lambda i, t: (0, 0)),
                pl.BlockSpec((slots, LANES), lambda i, t: (0, t[0] // per_block)),
            ],
            out_specs=pl.BlockSpec((rows, LANES), lambda i, t: (0, 0)),
            scratch_shapes=[pltpu.VMEM((width, width), BF16), pltpu.VMEM((rows, LANES), F32)],
        ),
        compiler_params=pltpu.CompilerParams(vmem_limit_bytes=32 * 2**20),
    )(tile.reshape(1), charges, skel_t)


def field_kernel(boxes, tile_ref, before, own, after, lists_ref, proxy_ref, out_ref, hot, picked, total):
    modes, targets, depth = proxy_ref.shape
    lists, tiles = lists_ref.shape
    groups = LANES // boxes
    cols = lists * tiles
    base = (tile_ref[0] - 1) * boxes
    hot[...] = jnp.zeros_like(hot)
    box = lax.broadcasted_iota(jnp.int32, (boxes, tiles), 0)
    for o in range(3):
        for l in range(lists):
            want = lists_ref[l : l + 1, :] - (base + o * boxes)
            block = jnp.where(box == want, 1.0, 0.0).astype(BF16)
            for u in range(groups):
                hot[
                    o * LANES + u * boxes : o * LANES + (u + 1) * boxes,
                    u * cols + l * tiles : u * cols + (l + 1) * tiles,
                ] = block
    source = jnp.concatenate([before[...], own[...], after[...]], axis=1)
    for h in range(groups // 2):
        got = jnp.dot(source, hot[:, 2 * h * cols : 2 * (h + 1) * cols], preferred_element_type=F32)
        got = got.reshape(modes, 2, SUBS, 2 * cols)
        for l in range(lists):
            low = got[..., l * tiles : (l + 1) * tiles]
            high = got[..., cols + l * tiles : cols + (l + 1) * tiles]
            both = jnp.concatenate([low, high], axis=2).astype(BF16)
            first = l * (groups * SUBS) + h * 2 * SUBS
            for c in range(2):
                picked[:, first : first + 2 * SUBS, c * tiles : (c + 1) * tiles] = both[:, c]
    stride = 2 * modes

    def one(m, carry):
        res = jnp.dot(proxy_ref[m], picked[m], preferred_element_type=F32)
        row = lax.rem(m, 2) * modes + (m // 2) * 2
        for c in range(2):
            total[pl.ds(row + c, targets, stride=stride), :] = res[:, c * tiles : (c + 1) * tiles]
        return carry

    lax.fori_loop(0, modes, one, 0, unroll=4)
    out_ref[...] = total[...].astype(BF16)


def fields(before, own, after, lists, proxy, tile, boxes):
    modes, targets, depth = proxy.shape
    rows = targets * 2 * modes
    groups = LANES // boxes
    tiles = lists.shape[1]

    def body(*refs):
        field_kernel(boxes, *refs)

    whole = pl.BlockSpec(memory_space=pltpu.VMEM)
    return pl.pallas_call(
        body,
        out_shape=jax.ShapeDtypeStruct((rows, tiles), BF16),
        in_specs=[pl.BlockSpec(memory_space=pltpu.SMEM)] + [whole] * 5,
        out_specs=whole,
        scratch_shapes=[
            pltpu.VMEM((3 * LANES, groups * lists.shape[0] * tiles), BF16),
            pltpu.VMEM((modes, depth, 2 * tiles), BF16),
            pltpu.VMEM((rows, tiles), F32),
        ],
        compiler_params=pltpu.CompilerParams(vmem_limit_bytes=40 * 2**20),
    )(tile.reshape(1), before, own, after, lists, proxy)


def synth_kernel(block_ref, table_ref, out_ref):
    peers, targets, rows, tiles = block_ref.shape
    half = rows // 2
    for p in range(targets):
        sums = []
        for parity in range(2):
            part = block_ref[:, p, parity * half : (parity + 1) * half, :].reshape(peers * half, tiles)
            weights = table_ref[parity * peers * half : (parity + 1) * peers * half, :]
            sums.append(
                lax.dot_general(part, weights, (((0,), (0,)), ((), ())), preferred_element_type=F32)
            )
        width = sums[0].shape[1]
        out_ref[p, :, :width] = (sums[0] + sums[1]).astype(BF16)
        out_ref[p, :, width:] = (sums[0] - sums[1]).astype(BF16)


def synthesis(block, table, step):
    peers, targets, rows, tiles = block.shape
    angles = 2 * table.shape[1]
    return pl.pallas_call(
        synth_kernel,
        out_shape=jax.ShapeDtypeStruct((targets, tiles, angles), BF16),
        grid=(targets // step,),
        in_specs=[
            pl.BlockSpec((peers, step, rows, tiles), lambda i: (0, i, 0, 0)),
            pl.BlockSpec(table.shape, lambda i: (0, 0)),
        ],
        out_specs=pl.BlockSpec((step, tiles, angles), lambda i: (i, 0, 0)),
        compiler_params=pltpu.CompilerParams(vmem_limit_bytes=32 * 2**20),
    )(block, table)


def shards(charges, proxy, tile_boxes, box_skel):
    modes_here, parts, skel_here = charges.shape
    _, targets, _ = proxy.shape
    tiles_here, _ = tile_boxes.shape
    slots = box_skel.shape[1]
    peers = lax.axis_size("mode")
    groups = lax.axis_size("tile")
    tile = lax.axis_index("tile").astype(jnp.int32)
    own = box_order(charges.reshape(modes_here * parts, skel_here), box_skel.T, tile)
    up = [(i, (i + 1) % groups) for i in range(groups)]
    before = lax.ppermute(own, "tile", up)
    after = lax.ppermute(own, "tile", [(j, i) for i, j in up])
    field = fields(before, own, after, tile_boxes.T, proxy, tile, skel_here // slots)
    width = targets // peers
    field = field.reshape(peers, width, modes_here * parts, tiles_here)
    block = lax.all_to_all(field, "mode", split_axis=0, concat_axis=0, tiled=True)
    table = half_table(modes_here * peers)
    return synthesis(block, table, 4)


def solution(mesh):
    placed = (P("mode", None, "tile"), P("mode", None, None), P("tile", None), P())
    return jax.shard_map(
        shards, mesh=mesh, in_specs=placed, out_specs=P("mode", "tile", None), check_vma=False
    )
```

```python
import math

import jax
import jax.numpy as jnp
from jax import lax
from jax.experimental import pallas as pl
from jax.experimental.pallas import tpu as pltpu
from jax.sharding import PartitionSpec as P

BF16 = jnp.bfloat16
F32 = jnp.float32
LANES = 128
SUBS = 8
ROWS16 = 16
MIB = 2**20


def half_table(modes):
    angles = 2 * modes
    row = lax.broadcasted_iota(jnp.int32, (2 * modes, modes), 0)
    angle = lax.broadcasted_iota(jnp.int32, (2 * modes, modes), 1)
    parity = row // modes
    rest = row % modes
    order = (rest // 2) * 2 + parity
    phase = (order * angle % angles).astype(F32) * (2.0 * math.pi / angles)
    weight = jnp.where(order == 0, 1.0, 2.0).astype(F32) / math.sqrt(2.0 * modes)
    return jnp.where(rest % 2 == 0, weight * jnp.cos(phase), -weight * jnp.sin(phase)).astype(BF16)


def order_kernel(boxes, charges_hbm, skel_hbm, out_ref, charges, skel, hot, rows, sems):
    modes, parts, width = charges.shape
    slots = skel.shape[0]
    tile = lax.axis_index("tile")
    per_block = LANES // boxes
    column = pl.multiple_of(tile // per_block * LANES, LANES)
    skel_copy = pltpu.make_async_copy(skel_hbm.at[:, pl.ds(column, LANES)], skel, sems.at[0])
    charges_copy = pltpu.make_async_copy(charges_hbm, charges, sems.at[1])
    skel_copy.start()
    charges_copy.start()
    spot = lax.broadcasted_iota(jnp.int32, (width, LANES), 0)
    lane = lax.broadcasted_iota(jnp.int32, (SUBS, LANES), 1)
    skel_copy.wait()
    index = jnp.zeros((SUBS, LANES), jnp.int32)
    for u in range(slots // SUBS):
        shift = lax.rem(u * boxes - lax.rem(tile, per_block) * boxes + LANES, LANES)
        moved = pltpu.roll(skel[u * SUBS : (u + 1) * SUBS, :], shift, 1)
        index = jnp.where(lane // boxes == u, moved, index)
    index = index - tile * width
    for q in range(SUBS):
        hot[:, q * LANES : (q + 1) * LANES] = jnp.where(spot == index[q : q + 1, :], 1.0, 0.0).astype(BF16)
    charges_copy.wait()
    count = modes * parts
    held = charges[...].reshape(count, width)
    moved = jnp.dot(held, hot[...], preferred_element_type=F32)
    for q in range(SUBS):
        rows[pl.ds(q, count, stride=SUBS), :] = moved[:, q * LANES : (q + 1) * LANES]
    out_ref[...] = rows[...].astype(BF16)


def box_order(charges, skel_t):
    modes, parts, width = charges.shape
    slots = skel_t.shape[0]
    boxes = width // slots
    rows = modes * parts * SUBS

    def body(*refs):
        order_kernel(boxes, *refs)

    return pl.pallas_call(
        body,
        out_shape=jax.ShapeDtypeStruct((rows, LANES), BF16),
        in_specs=[pl.BlockSpec(memory_space=pl.ANY)] * 2,
        out_specs=pl.BlockSpec(memory_space=pltpu.VMEM),
        scratch_shapes=[
            pltpu.VMEM((modes, parts, width), BF16),
            pltpu.VMEM((slots, LANES), jnp.int32),
            pltpu.VMEM((width, width), BF16),
            pltpu.VMEM((rows, LANES), F32),
            pltpu.SemaphoreType.DMA((2,)),
        ],
        compiler_params=pltpu.CompilerParams(vmem_limit_bytes=32 * MIB),
    )(charges, skel_t)


def field_kernel(boxes, near, own, far, lists_hbm, proxy_hbm, out_hbm, lists, proxy, hot, picked, field, sems):
    modes, targets, depth = proxy.shape
    count, tiles = lists.shape
    groups = LANES // boxes
    cols = count * tiles
    lists_copy = pltpu.make_async_copy(lists_hbm, lists, sems.at[0])
    proxy_copy = pltpu.make_async_copy(proxy_hbm, proxy, sems.at[1])
    lists_copy.start()
    proxy_copy.start()
    hot[...] = jnp.zeros_like(hot)
    tile = lax.axis_index("tile")
    toward = 1 - 2 * lax.rem(tile, 2)
    box = lax.broadcasted_iota(jnp.int32, (boxes, tiles), 0)
    lists_copy.wait()
    for o, owner in enumerate((tile + toward, tile, tile - toward)):
        for l in range(count):
            want = lists[l : l + 1, :] - owner * boxes
            block = jnp.where(box == want, 1.0, 0.0).astype(BF16)
            for u in range(groups):
                hot[
                    o * LANES + u * boxes : o * LANES + (u + 1) * boxes,
                    u * cols + l * tiles : u * cols + (l + 1) * tiles,
                ] = block
    source = jnp.concatenate([near[...], own[...], far[...]], axis=1)
    for h in range(groups // 2):
        got = jnp.dot(source, hot[:, 2 * h * cols : 2 * (h + 1) * cols], preferred_element_type=F32)
        got = got.reshape(modes, 2, SUBS, 2 * cols)
        for l in range(count):
            low = got[..., l * tiles : (l + 1) * tiles]
            high = got[..., cols + l * tiles : cols + (l + 1) * tiles]
            both = jnp.concatenate([low, high], axis=2).astype(BF16)
            first = l * (groups * SUBS) + h * 2 * SUBS
            for c in range(2):
                picked[:, first : first + 2 * SUBS, c * tiles : (c + 1) * tiles] = both[:, c]
    proxy_copy.wait()
    per = ROWS16 // 2
    half = modes // 2
    writes = []
    for g in range(modes // per):
        parts = []
        for j in range(per):
            m = g // (half // per) + 2 * (g % (half // per) * per + j)
            res = jnp.dot(proxy[m], picked[m], preferred_element_type=F32).astype(BF16)
            parts += [res[:, :tiles], res[:, tiles:]]
        span = slice(g * ROWS16, (g + 1) * ROWS16)
        field[:, span, :] = jnp.swapaxes(jnp.stack(parts, axis=0), 0, 1)
        copy = pltpu.make_async_copy(field.at[:, span, :], out_hbm.at[:, span, :], sems.at[2 + g])
        copy.start()
        writes.append(copy)
    for copy in writes:
        copy.wait()


def fields(near, own, far, lists, proxy, boxes):
    modes, targets, depth = proxy.shape
    count, tiles = lists.shape
    groups = LANES // boxes

    def body(*refs):
        field_kernel(boxes, *refs)

    held = pl.BlockSpec(memory_space=pltpu.VMEM)
    placed = pl.BlockSpec(memory_space=pl.ANY)
    shape = (targets, 2 * modes, tiles)
    return pl.pallas_call(
        body,
        out_shape=jax.ShapeDtypeStruct(shape, BF16),
        in_specs=[held] * 3 + [placed] * 2,
        out_specs=placed,
        scratch_shapes=[
            pltpu.VMEM((count, tiles), jnp.int32),
            pltpu.VMEM(proxy.shape, BF16),
            pltpu.VMEM((3 * LANES, groups * count * tiles), BF16),
            pltpu.VMEM((modes, depth, 2 * tiles), BF16),
            pltpu.VMEM(shape, BF16),
            pltpu.SemaphoreType.DMA((2 + 2 * modes // ROWS16,)),
        ],
        compiler_params=pltpu.CompilerParams(vmem_limit_bytes=40 * MIB),
    )(near, own, far, lists, proxy)


def synth_kernel(block_ref, table_ref, out_ref):
    peers, step, rows, tiles = block_ref.shape
    half = rows // 2
    depth = peers * half
    sums = []
    for parity in range(2):
        parts = [
            block_ref[:, p, parity * half : (parity + 1) * half, :].reshape(depth, tiles) for p in range(step)
        ]
        weights = table_ref[parity * depth : (parity + 1) * depth, :]
        sums.append(
            lax.dot_general(
                jnp.concatenate(parts, axis=1), weights, (((0,), (0,)), ((), ())), preferred_element_type=F32
            )
        )
    even, odd = sums
    width = even.shape[1]
    out_ref[:, :, :width] = (even + odd).astype(BF16).reshape(step, tiles, width)
    out_ref[:, :, width:] = (even - odd).astype(BF16).reshape(step, tiles, width)


def synthesis(block, table, step):
    peers, targets, rows, tiles = block.shape
    angles = 2 * table.shape[1]
    return pl.pallas_call(
        synth_kernel,
        out_shape=jax.ShapeDtypeStruct((targets, tiles, angles), BF16),
        grid=(targets // step,),
        in_specs=[
            pl.BlockSpec((peers, step, rows, tiles), lambda i: (0, i, 0, 0)),
            pl.BlockSpec(table.shape, lambda i: (0, 0)),
        ],
        out_specs=pl.BlockSpec((step, tiles, angles), lambda i: (i, 0, 0)),
        compiler_params=pltpu.CompilerParams(vmem_limit_bytes=40 * MIB),
    )(block, table)


def shards(charges, proxy, tile_boxes, box_skel):
    modes_here, parts, skel_here = charges.shape
    _, targets, _ = proxy.shape
    tiles_here, _ = tile_boxes.shape
    slots = box_skel.shape[1]
    peers = lax.axis_size("mode")
    groups = lax.axis_size("tile")
    own = box_order(charges, box_skel.T)
    far = lax.ppermute(own, "tile", [(i, (i - 1 + 2 * (i % 2)) % groups) for i in range(groups)])
    near = lax.ppermute(own, "tile", [(i, i + 1 - 2 * (i % 2)) for i in range(groups)])
    field = fields(near, own, far, tile_boxes.T, proxy, skel_here // slots)
    field = field.reshape(peers, targets // peers, modes_here * parts, tiles_here)
    block = lax.all_to_all(field, "mode", split_axis=0, concat_axis=0, tiled=True)
    table = half_table(modes_here * peers)
    return synthesis(block, table, 4)


def solution(mesh):
    placed = (P("mode", None, "tile"), P("mode", None, None), P("tile", None), P())
    return jax.shard_map(
        shards, mesh=mesh, in_specs=placed, out_specs=P("mode", "tile", None), check_vma=False
    )
```

```python
import math

import jax
import jax.numpy as jnp
from jax import lax
from jax.experimental import pallas as pl
from jax.experimental.pallas import tpu as pltpu
from jax.sharding import PartitionSpec as P

BF16 = jnp.bfloat16
F32 = jnp.float32
LANES = 128
SUBS = 8
ROWS16 = 16
MIB = 2**20
PIECES = 4


def half_table(modes):
    angles = 2 * modes
    row = lax.broadcasted_iota(jnp.int32, (2 * modes, modes), 0)
    angle = lax.broadcasted_iota(jnp.int32, (2 * modes, modes), 1)
    parity = row // modes
    rest = row % modes
    order = (rest // 2) * 2 + parity
    phase = (order * angle % angles).astype(F32) * (2.0 * math.pi / angles)
    weight = jnp.where(order == 0, 1.0, 2.0).astype(F32) / math.sqrt(2.0 * modes)
    return jnp.where(rest % 2 == 0, weight * jnp.cos(phase), -weight * jnp.sin(phase)).astype(BF16)


def one_hot_order(index, owner, hot):
    width = hot.shape[0]
    index = index - owner * width
    spot = lax.broadcasted_iota(jnp.int32, (SUBS, LANES), 0)
    for q in range(SUBS):
        low = index[q : q + 1, :] - spot
        for first in range(0, width, ROWS16):
            pair = [jnp.where(low == first + shift, 1.0, 0.0) for shift in (0, SUBS)]
            hot[first : first + ROWS16, q * LANES : (q + 1) * LANES] = jnp.concatenate(pair, axis=0).astype(BF16)


def box_rows(charges, hot, rows):
    modes, parts, width = charges.shape
    count = modes * parts
    moved = jnp.dot(charges[...].reshape(count, width), hot[...], preferred_element_type=F32)
    for q in range(SUBS):
        rows[pl.ds(q, count, stride=SUBS), :] = moved[:, q * LANES : (q + 1) * LANES]
    return rows[...].astype(BF16)


def owners():
    tile = lax.axis_index("tile")
    toward = 1 - 2 * lax.rem(tile, 2)
    return tile + toward, tile, tile - toward


def prepare_kernel(
    boxes,
    charges_hbm,
    skel_hbm,
    lists_hbm,
    proxy_hbm,
    order_ref,
    own_ref,
    pick_ref,
    proxy_ref,
    charges,
    skel,
    lists,
    hot,
    rows,
    sems,
):
    slots = skel.shape[1]
    count, tiles = lists.shape
    cols = count * tiles
    groups = LANES // boxes
    total = skel_hbm.shape[1] // boxes
    places = [jnp.clip(owner, 0, total - 1) for owner in owners()]
    copies = []
    for o, place in enumerate(places):
        column = pl.multiple_of(place // groups * LANES, LANES)
        copies.append(pltpu.make_async_copy(skel_hbm.at[:, pl.ds(column, LANES)], skel.at[o], sems.at[o]))
    copies.append(pltpu.make_async_copy(charges_hbm, charges, sems.at[3]))
    copies.append(pltpu.make_async_copy(lists_hbm, lists, sems.at[4]))
    for copy in copies:
        copy.start()
    modes = proxy_hbm.shape[0]
    per = modes // PIECES
    fetches = []
    for k in range(PIECES):
        span = pl.ds(k * per, per)
        fetches.append(pltpu.make_async_copy(proxy_hbm.at[span], proxy_ref.at[span], sems.at[5 + k]))
        fetches[-1].start()
    pick_ref[...] = jnp.zeros_like(pick_ref)
    for copy in copies:
        copy.wait()
    lane = lax.broadcasted_iota(jnp.int32, (SUBS, LANES), 1)
    for o in (1, 0, 2):
        index = jnp.zeros((SUBS, LANES), jnp.int32)
        for u in range(slots // SUBS):
            shift = lax.rem(u * boxes - lax.rem(places[o], groups) * boxes + LANES, LANES)
            moved = pltpu.roll(skel[o, u * SUBS : (u + 1) * SUBS, :], shift, 1)
            index = jnp.where(lane // boxes == u, moved, index)
        one_hot_order(index, places[o], hot if o == 1 else order_ref.at[o // 2])
        if o == 1:
            own_ref[...] = box_rows(charges, hot, rows)
    box = lax.broadcasted_iota(jnp.int32, (boxes, tiles), 0)
    for o, owner in enumerate(owners()):
        for l in range(count):
            block = jnp.where(box == lists[l : l + 1, :] - owner * boxes, 1.0, 0.0).astype(BF16)
            for u in range(groups):
                pick_ref[
                    o * LANES + u * boxes : o * LANES + (u + 1) * boxes,
                    u * cols + l * tiles : u * cols + (l + 1) * tiles,
                ] = block
    for fetch in fetches:
        fetch.wait()


def prepare(charges, skel_t, lists, proxy):
    modes, parts, width = charges.shape
    slots = skel_t.shape[0]
    boxes = width // slots
    count, tiles = lists.shape
    rows = modes * parts * SUBS

    def body(*refs):
        prepare_kernel(boxes, *refs)

    held = pl.BlockSpec(memory_space=pltpu.VMEM)
    return pl.pallas_call(
        body,
        out_shape=[
            pltpu.VMEM((2, width, width), BF16),
            pltpu.VMEM((rows, LANES), BF16),
            pltpu.VMEM((3 * LANES, LANES // boxes * count * tiles), BF16),
            pltpu.VMEM(proxy.shape, BF16),
        ],
        in_specs=[pl.BlockSpec(memory_space=pltpu.HBM)] * 4,
        out_specs=[held] * 4,
        scratch_shapes=[
            pltpu.VMEM(charges.shape, BF16),
            pltpu.VMEM((3, slots, LANES), jnp.int32),
            pltpu.VMEM((count, tiles), jnp.int32),
            pltpu.VMEM((width, width), BF16),
            pltpu.VMEM((rows, LANES), F32),
            pltpu.SemaphoreType.DMA((5 + PIECES,)),
        ],
        compiler_params=pltpu.CompilerParams(vmem_limit_bytes=24 * MIB),
    )(*(pltpu.with_memory_space_constraint(x, pltpu.HBM) for x in (charges, skel_t, lists, proxy)))


def field_kernel(groups, tiles, near, own, far, order, pick, proxy, out_hbm, picked, field, rows, sems):
    modes, targets, depth = proxy.shape
    cols = pick.shape[1] // groups
    count = cols // tiles
    source = jnp.concatenate(
        [box_rows(near, order.at[0], rows.at[0]), own[...], box_rows(far, order.at[1], rows.at[1])], axis=1
    )
    for h in range(groups // 2):
        got = jnp.dot(source, pick[:, 2 * h * cols : 2 * (h + 1) * cols], preferred_element_type=F32)
        got = got.reshape(modes, 2, SUBS, 2 * cols)
        for l in range(count):
            low = got[..., l * tiles : (l + 1) * tiles]
            high = got[..., cols + l * tiles : cols + (l + 1) * tiles]
            both = jnp.concatenate([low, high], axis=2).astype(BF16)
            first = l * (groups * SUBS) + h * 2 * SUBS
            for c in range(2):
                picked[:, first : first + 2 * SUBS, c * tiles : (c + 1) * tiles] = both[:, c]
    per = ROWS16 // 2
    half = modes // 2
    writes = []
    for g in range(modes // per):
        parts = []
        for j in range(per):
            m = g // (half // per) + 2 * (g % (half // per) * per + j)
            res = jnp.dot(proxy[m], picked[m], preferred_element_type=F32).astype(BF16)
            parts += [res[:, :tiles], res[:, tiles:]]
        span = slice(g * ROWS16, (g + 1) * ROWS16)
        wide = targets // PIECES
        for k in range(PIECES):
            chunk = slice(k * wide, (k + 1) * wide)
            stack = jnp.stack([part[chunk] for part in parts], axis=0)
            field[chunk, span, :] = jnp.swapaxes(stack, 0, 1)
            copy = pltpu.make_async_copy(
                field.at[chunk, span, :], out_hbm.at[chunk, span, :], sems.at[g * PIECES + k]
            )
            copy.start()
            writes.append(copy)
    for copy in writes:
        copy.wait()


def fields(near, own, far, order, pick, proxy, boxes, tiles):
    modes, targets, depth = proxy.shape
    groups = LANES // boxes

    def body(*refs):
        field_kernel(groups, tiles, *refs)

    held = pl.BlockSpec(memory_space=pltpu.VMEM)
    placed = pl.BlockSpec(memory_space=pltpu.HBM)
    shape = (targets, 2 * modes, tiles)
    return pl.pallas_call(
        body,
        out_shape=pltpu.HBM(shape, BF16),
        in_specs=[held] * 6,
        out_specs=placed,
        scratch_shapes=[
            pltpu.VMEM((modes, depth, 2 * tiles), BF16),
            pltpu.VMEM(shape, BF16),
            pltpu.VMEM((2,) + own.shape, F32),
            pltpu.SemaphoreType.DMA((2 * modes // ROWS16 * PIECES,)),
        ],
        compiler_params=pltpu.CompilerParams(vmem_limit_bytes=32 * MIB),
    )(near, own, far, order, pick, proxy)


def synth_kernel(step, block_hbm, table_hbm, out_hbm, block, table, out, sems):
    peers, targets, rows, tiles = block.shape
    half = rows // 2
    depth = peers * half
    width = table.shape[1]
    chunks = targets // step
    table_copy = pltpu.make_async_copy(table_hbm, table, sems.at[2 * chunks])
    reads = []
    for k in range(chunks):
        span = pl.ds(k * step, step)
        reads.append(pltpu.make_async_copy(block_hbm.at[:, span], block.at[:, span], sems.at[k]))
        reads[-1].start()
        if k == 0:
            table_copy.start()
    table_copy.wait()
    writes = []
    for k in range(chunks):
        reads[k].wait()
        sums = []
        for parity in range(2):
            parts = [
                block[:, k * step + p, parity * half : (parity + 1) * half, :].reshape(depth, tiles)
                for p in range(step)
            ]
            weights = table[parity * depth : (parity + 1) * depth, :]
            sums.append(
                lax.dot_general(
                    jnp.concatenate(parts, axis=1), weights, (((0,), (0,)), ((), ())), preferred_element_type=F32
                )
            )
        even, odd = sums
        span = slice(k * step, (k + 1) * step)
        out[span, :, :width] = (even + odd).astype(BF16).reshape(step, tiles, width)
        out[span, :, width:] = (even - odd).astype(BF16).reshape(step, tiles, width)
        writes.append(pltpu.make_async_copy(out.at[span], out_hbm.at[span], sems.at[chunks + k]))
        writes[-1].start()
    for copy in writes:
        copy.wait()


def synthesis(block, table, step):
    peers, targets, rows, tiles = block.shape
    angles = 2 * table.shape[1]
    shape = (targets, tiles, angles)

    def body(*refs):
        synth_kernel(step, *refs)

    placed = pl.BlockSpec(memory_space=pltpu.HBM)
    return pl.pallas_call(
        body,
        out_shape=pltpu.HBM(shape, BF16),
        in_specs=[placed] * 2,
        out_specs=placed,
        scratch_shapes=[
            pltpu.VMEM(block.shape, BF16),
            pltpu.VMEM(table.shape, BF16),
            pltpu.VMEM(shape, BF16),
            pltpu.SemaphoreType.DMA((2 * targets // step + 1,)),
        ],
        compiler_params=pltpu.CompilerParams(vmem_limit_bytes=40 * MIB),
    )(*(pltpu.with_memory_space_constraint(x, pltpu.HBM) for x in (block, table)))


def shards(charges, proxy, tile_boxes, box_skel):
    modes_here, parts, skel_here = charges.shape
    _, targets, _ = proxy.shape
    tiles_here, _ = tile_boxes.shape
    slots = box_skel.shape[1]
    peers = lax.axis_size("mode")
    groups = lax.axis_size("tile")
    far = lax.ppermute(charges, "tile", [(i, (i - 1 + 2 * (i % 2)) % groups) for i in range(groups)])
    near = lax.ppermute(charges, "tile", [(i, i + 1 - 2 * (i % 2)) for i in range(groups)])
    order, own, pick, proxy = prepare(charges, box_skel.T, tile_boxes.T, proxy)
    field = fields(near, own, far, order, pick, proxy, skel_here // slots, tiles_here)
    field = field.reshape(peers, targets // peers, modes_here * parts, tiles_here)
    block = lax.all_to_all(field, "mode", split_axis=0, concat_axis=0, tiled=True)
    table = half_table(modes_here * peers)
    return synthesis(block, table, 4)


def solution(mesh):
    placed = (P("mode", None, "tile"), P("mode", None, None), P("tile", None), P())
    return jax.shard_map(
        shards, mesh=mesh, in_specs=placed, out_specs=P("mode", "tile", None), check_vma=False
    )
```

```python
import math

import jax
import jax.numpy as jnp
import ml_dtypes
import numpy as np
from jax import lax
from jax.experimental import pallas as pl
from jax.experimental.pallas import tpu as pltpu
from jax.sharding import PartitionSpec as P

BF16 = jnp.bfloat16
F32 = jnp.float32
LANES = 128
SUBS = 8
ROWS16 = 16
MIB = 2**20
PIECES = 4
STEPS = (2, 2, 4, 4, 2, 2)


def half_table(modes):
    angles = 2 * modes
    rest = np.arange(2 * modes) % modes
    order = (rest // 2) * 2 + np.arange(2 * modes) // modes
    phase = (order[:, None] * np.arange(modes)[None, :] % angles).astype(np.float32)
    phase = phase * np.float32(2.0 * math.pi / angles)
    weight = np.where(order == 0, 1.0, 2.0).astype(np.float32) / np.float32(math.sqrt(2.0 * modes))
    wave = np.where((rest % 2 == 0)[:, None], np.cos(phase), -np.sin(phase)).astype(np.float32)
    return jnp.asarray((weight[:, None] * wave).astype(ml_dtypes.bfloat16))


def one_hot_order(index, owner, hot):
    width = hot.shape[0]
    index = index - owner * width
    spot = lax.broadcasted_iota(jnp.int32, (SUBS, LANES), 0)
    for q in range(SUBS):
        low = index[q : q + 1, :] - spot
        for first in range(0, width, ROWS16):
            pair = [jnp.where(low == first + shift, 1.0, 0.0) for shift in (0, SUBS)]
            hot[first : first + ROWS16, q * LANES : (q + 1) * LANES] = jnp.concatenate(pair, axis=0).astype(BF16)


def box_rows(charges, hot, rows):
    modes, parts, width = charges.shape
    count = modes * parts
    moved = jnp.dot(charges[...].reshape(count, width), hot[...], preferred_element_type=F32)
    for q in range(SUBS):
        rows[pl.ds(q, count, stride=SUBS), :] = moved[:, q * LANES : (q + 1) * LANES]
    return rows[...].astype(BF16)


def owners():
    tile = lax.axis_index("tile")
    toward = 1 - 2 * lax.rem(tile, 2)
    return tile + toward, tile, tile - toward


def lane_slot(o, u, groups):
    return (u + groups // 2) % groups if o == 1 else u


def prepare_kernel(
    boxes,
    charges_hbm,
    skel_hbm,
    lists_hbm,
    proxy_hbm,
    order_ref,
    own_ref,
    pick_ref,
    proxy_ref,
    charges,
    skel,
    lists,
    hot,
    rows,
    sems,
):
    slots = skel.shape[1]
    count, tiles = lists.shape
    cols = count * tiles
    groups = LANES // boxes
    total = skel_hbm.shape[1] // boxes
    places = [jnp.clip(owner, 0, total - 1) for owner in owners()]
    copies = []
    for o, place in enumerate(places):
        column = pl.multiple_of(place // groups * LANES, LANES)
        copies.append(pltpu.make_async_copy(skel_hbm.at[:, pl.ds(column, LANES)], skel.at[o], sems.at[o]))
    copies.append(pltpu.make_async_copy(charges_hbm, charges, sems.at[3]))
    copies.append(pltpu.make_async_copy(lists_hbm, lists, sems.at[4]))
    for copy in copies:
        copy.start()
    modes = proxy_hbm.shape[0]
    per = modes // PIECES
    fetches = []
    for k in range(PIECES):
        span = pl.ds(k * per, per)
        fetches.append(pltpu.make_async_copy(proxy_hbm.at[span], proxy_ref.at[span], sems.at[5 + k]))
        fetches[-1].start()
    pick_ref[...] = jnp.zeros_like(pick_ref)
    for copy in copies:
        copy.wait()
    lane = lax.broadcasted_iota(jnp.int32, (SUBS, LANES), 1)
    for o in (1, 0, 2):
        index = jnp.zeros((SUBS, LANES), jnp.int32)
        for u in range(slots // SUBS):
            v = lane_slot(o, u, groups)
            shift = lax.rem(v * boxes - lax.rem(places[o], groups) * boxes + LANES, LANES)
            moved = pltpu.roll(skel[o, u * SUBS : (u + 1) * SUBS, :], shift, 1)
            index = jnp.where(lane // boxes == v, moved, index)
        one_hot_order(index, places[o], hot if o == 1 else order_ref.at[o // 2])
        if o == 1:
            own_ref[...] = box_rows(charges, hot, rows)
    box = lax.broadcasted_iota(jnp.int32, (boxes, tiles), 0)
    for o, owner in enumerate(owners()):
        for l in range(count):
            block = jnp.where(box == lists[l : l + 1, :] - owner * boxes, 1.0, 0.0).astype(BF16)
            for u in range(groups):
                first = o // 2 * LANES + lane_slot(o, u, groups) * boxes
                pick_ref[first : first + boxes, u * cols + l * tiles : u * cols + (l + 1) * tiles] = block
    for fetch in fetches:
        fetch.wait()


def prepare(charges, skel_t, lists, proxy):
    modes, parts, width = charges.shape
    slots = skel_t.shape[0]
    boxes = width // slots
    count, tiles = lists.shape
    rows = modes * parts * SUBS

    def body(*refs):
        prepare_kernel(boxes, *refs)

    held = pl.BlockSpec(memory_space=pltpu.VMEM)
    return pl.pallas_call(
        body,
        out_shape=[
            pltpu.VMEM((2, width, width), BF16),
            pltpu.VMEM((rows, LANES), BF16),
            pltpu.VMEM((2 * LANES, LANES // boxes * count * tiles), BF16),
            pltpu.VMEM(proxy.shape, BF16),
        ],
        in_specs=[pl.BlockSpec(memory_space=pltpu.HBM)] * 4,
        out_specs=[held] * 4,
        scratch_shapes=[
            pltpu.VMEM(charges.shape, BF16),
            pltpu.VMEM((3, slots, LANES), jnp.int32),
            pltpu.VMEM((count, tiles), jnp.int32),
            pltpu.VMEM((width, width), BF16),
            pltpu.VMEM((rows, LANES), F32),
            pltpu.SemaphoreType.DMA((5 + PIECES,)),
        ],
        compiler_params=pltpu.CompilerParams(vmem_limit_bytes=24 * MIB),
    )(*(pltpu.with_memory_space_constraint(x, pltpu.HBM) for x in (charges, skel_t, lists, proxy)))


def field_kernel(groups, tiles, near, own, far, order, pick, proxy, field, picked, rows):
    modes, targets, depth = proxy.shape
    cols = pick.shape[1] // groups
    count = cols // tiles
    first_rows = box_rows(near, order.at[0], rows.at[0])
    last_rows = box_rows(far, order.at[1], rows.at[1])
    own_rows = own[...]
    low_half = lax.broadcasted_iota(jnp.int32, own_rows.shape, 1) < LANES // 2
    for h in range(groups // 2):
        mixed = jnp.where(low_half, first_rows, own_rows) if h == 0 else jnp.where(low_half, own_rows, first_rows)
        source = jnp.concatenate([mixed, last_rows], axis=1)
        got = jnp.dot(source, pick[:, 2 * h * cols : 2 * (h + 1) * cols], preferred_element_type=F32)
        got = got.reshape(modes, 2, SUBS, 2 * cols)
        for l in range(count):
            low = got[..., l * tiles : (l + 1) * tiles]
            high = got[..., cols + l * tiles : cols + (l + 1) * tiles]
            both = jnp.concatenate([low, high], axis=2).astype(BF16)
            first = l * (groups * SUBS) + h * 2 * SUBS
            for c in range(2):
                picked[:, first : first + 2 * SUBS, c * tiles : (c + 1) * tiles] = both[:, c]
    per = ROWS16 // 2
    half = modes // 2
    for g in range(modes // per):
        parts = []
        for j in range(per):
            m = g // (half // per) + 2 * (g % (half // per) * per + j)
            res = jnp.dot(proxy[m], picked[m], preferred_element_type=F32).astype(BF16)
            parts += [res[:, :tiles], res[:, tiles:]]
        span = slice(g * ROWS16, (g + 1) * ROWS16)
        wide = targets // PIECES
        for k in range(PIECES):
            chunk = slice(k * wide, (k + 1) * wide)
            stack = jnp.stack([part[chunk] for part in parts], axis=0)
            field[chunk, span, :] = jnp.swapaxes(stack, 0, 1)


def fields(near, own, far, order, pick, proxy, boxes, tiles):
    modes, targets, depth = proxy.shape
    groups = LANES // boxes

    def body(*refs):
        field_kernel(groups, tiles, *refs)

    held = pl.BlockSpec(memory_space=pltpu.VMEM)
    shape = (targets, 2 * modes, tiles)
    return pl.pallas_call(
        body,
        out_shape=pltpu.VMEM(shape, BF16),
        in_specs=[held] * 6,
        out_specs=held,
        scratch_shapes=[
            pltpu.VMEM((modes, depth, 2 * tiles), BF16),
            pltpu.VMEM((2,) + own.shape, F32),
        ],
        compiler_params=pltpu.CompilerParams(vmem_limit_bytes=32 * MIB),
    )(near, own, far, order, pick, proxy)


def synth_kernel(spans, block, table, out_hbm, out, sems):
    peers, targets, rows, tiles = block.shape
    half = rows // 2
    depth = peers * half
    width = table.shape[1]
    writes = []
    for k, (lo, hi) in enumerate(spans):
        sums = []
        for parity in range(2):
            parts = [
                block[:, p, parity * half : (parity + 1) * half, :].reshape(depth, tiles) for p in range(lo, hi)
            ]
            weights = table[parity * depth : (parity + 1) * depth, :]
            sums.append(
                lax.dot_general(
                    jnp.concatenate(parts, axis=1), weights, (((0,), (0,)), ((), ())), preferred_element_type=F32
                )
            )
        even, odd = sums
        out[lo:hi, :, :width] = (even + odd).astype(BF16).reshape(hi - lo, tiles, width)
        out[lo:hi, :, width:] = (even - odd).astype(BF16).reshape(hi - lo, tiles, width)
        writes.append(pltpu.make_async_copy(out.at[lo:hi], out_hbm.at[lo:hi], sems.at[k]))
        writes[-1].start()
    for copy in writes:
        copy.wait()


def synthesis(block, table, steps):
    peers, targets, rows, tiles = block.shape
    angles = 2 * table.shape[1]
    shape = (targets, tiles, angles)
    ends = [sum(steps[: k + 1]) for k in range(len(steps))]
    spans = list(zip([0] + ends[:-1], ends))

    def body(*refs):
        synth_kernel(spans, *refs)

    placed = pl.BlockSpec(memory_space=pltpu.HBM)
    return pl.pallas_call(
        body,
        out_shape=pltpu.HBM(shape, BF16),
        in_specs=[pl.BlockSpec(memory_space=pltpu.VMEM)] * 2,
        out_specs=placed,
        scratch_shapes=[
            pltpu.VMEM(shape, BF16),
            pltpu.SemaphoreType.DMA((len(spans),)),
        ],
        compiler_params=pltpu.CompilerParams(vmem_limit_bytes=16 * MIB),
        cost_estimate=pl.CostEstimate(flops=2**32, bytes_accessed=2**24, transcendentals=0),
    )(pltpu.with_memory_space_constraint(block, pltpu.VMEM), table)


def shards(charges, proxy, tile_boxes, box_skel):
    modes_here, parts, skel_here = charges.shape
    _, targets, _ = proxy.shape
    tiles_here, _ = tile_boxes.shape
    slots = box_skel.shape[1]
    peers = lax.axis_size("mode")
    groups = lax.axis_size("tile")
    far = lax.ppermute(charges, "tile", [(i, (i - 1 + 2 * (i % 2)) % groups) for i in range(groups)])
    near = lax.ppermute(charges, "tile", [(i, i + 1 - 2 * (i % 2)) for i in range(groups)])
    order, own, pick, proxy = prepare(charges, box_skel.T, tile_boxes.T, proxy)
    field = fields(near, own, far, order, pick, proxy, skel_here // slots, tiles_here)
    field = field.reshape(peers, targets // peers, modes_here * parts, tiles_here)
    block = lax.all_to_all(field, "mode", split_axis=0, concat_axis=0, tiled=True)
    table = half_table(modes_here * peers)
    return synthesis(block, table, STEPS)


def solution(mesh):
    placed = (P("mode", None, "tile"), P("mode", None, None), P("tile", None), P())
    return jax.shard_map(
        shards, mesh=mesh, in_specs=placed, out_specs=P("mode", "tile", None), check_vma=False
    )
```

```python
import math

import jax
import jax.numpy as jnp
import ml_dtypes
import numpy as np
from jax import lax
from jax.experimental import pallas as pl
from jax.experimental.pallas import tpu as pltpu
from jax.sharding import PartitionSpec as P

BF16 = jnp.bfloat16
F32 = jnp.float32
LANES = 128
SUBS = 8
ROWS16 = 16
MIB = 2**20
PIECES = 4
STEPS = (2, 2, 4, 4, 2, 2)


def half_table(modes):
    angles = 2 * modes
    rest = np.arange(2 * modes) % modes
    order = (rest // 2) * 2 + np.arange(2 * modes) // modes
    phase = (order[:, None] * np.arange(modes)[None, :] % angles).astype(np.float32)
    phase = phase * np.float32(2.0 * math.pi / angles)
    weight = np.where(order == 0, 1.0, 2.0).astype(np.float32) / np.float32(math.sqrt(2.0 * modes))
    wave = np.where((rest % 2 == 0)[:, None], np.cos(phase), -np.sin(phase)).astype(np.float32)
    return jnp.asarray((weight[:, None] * wave).astype(ml_dtypes.bfloat16))


def one_hot_order(index, owner, hot):
    width = hot.shape[0]
    index = index - owner * width
    spot = lax.broadcasted_iota(jnp.int32, (SUBS, LANES), 0)
    for q in range(SUBS):
        low = index[q : q + 1, :] - spot
        for first in range(0, width, ROWS16):
            pair = [jnp.where(low == first + shift, 1.0, 0.0) for shift in (0, SUBS)]
            hot[first : first + ROWS16, q * LANES : (q + 1) * LANES] = jnp.concatenate(pair, axis=0).astype(BF16)


def box_rows(charges, hot, rows):
    modes, parts, width = charges.shape
    count = modes * parts
    moved = jnp.dot(charges[...].reshape(count, width), hot[...], preferred_element_type=F32)
    for q in range(SUBS):
        rows[pl.ds(q, count, stride=SUBS), :] = moved[:, q * LANES : (q + 1) * LANES]
    return rows[...].astype(BF16)


def owners():
    tile = lax.axis_index("tile")
    toward = 1 - 2 * lax.rem(tile, 2)
    return tile + toward, tile, tile - toward


def lane_slot(o, u, groups):
    return (u + groups // 2) % groups if o == 1 else u


def prepare_kernel(
    boxes,
    charges_hbm,
    skel_hbm,
    lists_hbm,
    proxy_hbm,
    order_ref,
    own_ref,
    pick_ref,
    proxy_ref,
    charges,
    skel,
    lists,
    hot,
    rows,
    sems,
):
    slots = skel.shape[1]
    count, tiles = lists.shape
    cols = count * tiles
    groups = LANES // boxes
    total = skel_hbm.shape[1] // boxes
    places = [jnp.clip(owner, 0, total - 1) for owner in owners()]
    copies = []
    for o, place in enumerate(places):
        column = pl.multiple_of(place // groups * LANES, LANES)
        copies.append(pltpu.make_async_copy(skel_hbm.at[:, pl.ds(column, LANES)], skel.at[o], sems.at[o]))
    copies.append(pltpu.make_async_copy(charges_hbm, charges, sems.at[3]))
    copies.append(pltpu.make_async_copy(lists_hbm, lists, sems.at[4]))
    for copy in copies:
        copy.start()
    modes = proxy_hbm.shape[0]
    per = modes // PIECES
    fetches = []
    for k in range(PIECES):
        span = pl.ds(k * per, per)
        fetches.append(pltpu.make_async_copy(proxy_hbm.at[span], proxy_ref.at[span], sems.at[5 + k]))
        fetches[-1].start()
    pick_ref[...] = jnp.zeros_like(pick_ref)
    for copy in copies:
        copy.wait()
    lane = lax.broadcasted_iota(jnp.int32, (SUBS, LANES), 1)
    for o in (1, 0, 2):
        index = jnp.zeros((SUBS, LANES), jnp.int32)
        for u in range(slots // SUBS):
            v = lane_slot(o, u, groups)
            shift = lax.rem(v * boxes - lax.rem(places[o], groups) * boxes + LANES, LANES)
            moved = pltpu.roll(skel[o, u * SUBS : (u + 1) * SUBS, :], shift, 1)
            index = jnp.where(lane // boxes == v, moved, index)
        one_hot_order(index, places[o], hot if o == 1 else order_ref.at[o // 2])
        if o == 1:
            own_ref[...] = box_rows(charges, hot, rows)
    box = lax.broadcasted_iota(jnp.int32, (boxes, tiles), 0)
    for o, owner in enumerate(owners()):
        for l in range(count):
            block = jnp.where(box == lists[l : l + 1, :] - owner * boxes, 1.0, 0.0).astype(BF16)
            for u in range(groups):
                first = o // 2 * LANES + lane_slot(o, u, groups) * boxes
                pick_ref[first : first + boxes, u * cols + l * tiles : u * cols + (l + 1) * tiles] = block
    for fetch in fetches:
        fetch.wait()


def prepare(charges, skel_t, lists, proxy):
    modes, parts, width = charges.shape
    slots = skel_t.shape[0]
    boxes = width // slots
    count, tiles = lists.shape
    rows = modes * parts * SUBS

    def body(*refs):
        prepare_kernel(boxes, *refs)

    held = pl.BlockSpec(memory_space=pltpu.VMEM)
    return pl.pallas_call(
        body,
        out_shape=[
            pltpu.VMEM((2, width, width), BF16),
            pltpu.VMEM((rows, LANES), BF16),
            pltpu.VMEM((2 * LANES, LANES // boxes * count * tiles), BF16),
            pltpu.VMEM(proxy.shape, BF16),
        ],
        in_specs=[pl.BlockSpec(memory_space=pltpu.HBM)] * 4,
        out_specs=[held] * 4,
        scratch_shapes=[
            pltpu.VMEM(charges.shape, BF16),
            pltpu.VMEM((3, slots, LANES), jnp.int32),
            pltpu.VMEM((count, tiles), jnp.int32),
            pltpu.VMEM((width, width), BF16),
            pltpu.VMEM((rows, LANES), F32),
            pltpu.SemaphoreType.DMA((5 + PIECES,)),
        ],
        compiler_params=pltpu.CompilerParams(vmem_limit_bytes=24 * MIB),
    )(*(pltpu.with_memory_space_constraint(x, pltpu.HBM) for x in (charges, skel_t, lists, proxy)))


def field_kernel(groups, tiles, near, own, far, order, pick, proxy, field, picked, rows):
    modes, targets, depth = proxy.shape
    cols = pick.shape[1] // groups
    count = cols // tiles
    first_rows = box_rows(near, order.at[0], rows.at[0])
    last_rows = box_rows(far, order.at[1], rows.at[1])
    own_rows = own[...]
    low_half = lax.broadcasted_iota(jnp.int32, own_rows.shape, 1) < LANES // 2
    for h in range(groups // 2):
        mixed = jnp.where(low_half, first_rows, own_rows) if h == 0 else jnp.where(low_half, own_rows, first_rows)
        source = jnp.concatenate([mixed, last_rows], axis=1)
        got = jnp.dot(source, pick[:, 2 * h * cols : 2 * (h + 1) * cols], preferred_element_type=F32)
        got = got.reshape(modes, 2, SUBS, 2 * cols)
        for l in range(count):
            low = got[..., l * tiles : (l + 1) * tiles]
            high = got[..., cols + l * tiles : cols + (l + 1) * tiles]
            both = jnp.concatenate([low, high], axis=2).astype(BF16)
            first = l * (groups * SUBS) + h * 2 * SUBS
            for c in range(2):
                picked[:, first : first + 2 * SUBS, c * tiles : (c + 1) * tiles] = both[:, c]
    per = ROWS16 // 2
    half = modes // 2
    for g in range(modes // per):
        parts = []
        for j in range(per):
            m = g // (half // per) + 2 * (g % (half // per) * per + j)
            res = jnp.dot(proxy[m], picked[m], preferred_element_type=F32).astype(BF16)
            parts += [res[:, :tiles], res[:, tiles:]]
        span = slice(g * ROWS16, (g + 1) * ROWS16)
        wide = targets // PIECES
        for k in range(PIECES):
            chunk = slice(k * wide, (k + 1) * wide)
            stack = jnp.stack([part[chunk] for part in parts], axis=0)
            field[chunk, span, :] = jnp.swapaxes(stack, 0, 1)


def fields(near, own, far, order, pick, proxy, boxes, tiles):
    modes, targets, depth = proxy.shape
    groups = LANES // boxes

    def body(*refs):
        field_kernel(groups, tiles, *refs)

    held = pl.BlockSpec(memory_space=pltpu.VMEM)
    shape = (targets, 2 * modes, tiles)
    return pl.pallas_call(
        body,
        out_shape=pltpu.VMEM(shape, BF16),
        in_specs=[held] * 6,
        out_specs=held,
        scratch_shapes=[
            pltpu.VMEM((modes, depth, 2 * tiles), BF16),
            pltpu.VMEM((2,) + own.shape, F32),
        ],
        compiler_params=pltpu.CompilerParams(vmem_limit_bytes=32 * MIB),
    )(near, own, far, order, pick, proxy)


def synth_kernel(spans, block, table, out_hbm, out, sems):
    peers, targets, rows, tiles = block.shape
    half = rows // 2
    depth = peers * half
    width = table.shape[1]
    writes = []
    for k, (lo, hi) in enumerate(spans):
        sums = []
        for parity in range(2):
            parts = [
                block[:, p, parity * half : (parity + 1) * half, :].reshape(depth, tiles) for p in range(lo, hi)
            ]
            weights = table[parity * depth : (parity + 1) * depth, :]
            sums.append(
                lax.dot_general(
                    jnp.concatenate(parts, axis=1), weights, (((0,), (0,)), ((), ())), preferred_element_type=F32
                )
            )
        even, odd = sums
        out[lo:hi, :, :width] = (even + odd).astype(BF16).reshape(hi - lo, tiles, width)
        out[lo:hi, :, width:] = (even - odd).astype(BF16).reshape(hi - lo, tiles, width)
        writes.append(pltpu.make_async_copy(out.at[lo:hi], out_hbm.at[lo:hi], sems.at[k]))
        writes[-1].start()
    for copy in writes:
        copy.wait()


def synthesis(block, table, steps):
    peers, targets, rows, tiles = block.shape
    angles = 2 * table.shape[1]
    shape = (targets, tiles, angles)
    ends = [sum(steps[: k + 1]) for k in range(len(steps))]
    spans = list(zip([0] + ends[:-1], ends))

    def body(*refs):
        synth_kernel(spans, *refs)

    placed = pl.BlockSpec(memory_space=pltpu.HBM)
    return pl.pallas_call(
        body,
        out_shape=pltpu.HBM(shape, BF16),
        in_specs=[pl.BlockSpec(memory_space=pltpu.VMEM)] * 2,
        out_specs=placed,
        scratch_shapes=[
            pltpu.VMEM(shape, BF16),
            pltpu.SemaphoreType.DMA((len(spans),)),
        ],
        compiler_params=pltpu.CompilerParams(vmem_limit_bytes=16 * MIB),
        cost_estimate=pl.CostEstimate(flops=2**32, bytes_accessed=2**24, transcendentals=0),
    )(pltpu.with_memory_space_constraint(block, pltpu.VMEM), table)


def shards(charges, proxy, tile_boxes, box_skel):
    modes_here, parts, skel_here = charges.shape
    _, targets, _ = proxy.shape
    tiles_here, _ = tile_boxes.shape
    slots = box_skel.shape[1]
    peers = lax.axis_size("mode")
    groups = lax.axis_size("tile")
    far = lax.ppermute(charges, "tile", [(i, i - 1 + 2 * (i % 2)) for i in range(1, groups - 1)])
    near = lax.ppermute(charges, "tile", [(i, i + 1 - 2 * (i % 2)) for i in range(groups)])
    order, own, pick, proxy = prepare(charges, box_skel.T, tile_boxes.T, proxy)
    field = fields(near, own, far, order, pick, proxy, skel_here // slots, tiles_here)
    field = field.reshape(peers, targets // peers, modes_here * parts, tiles_here)
    block = lax.all_to_all(field, "mode", split_axis=0, concat_axis=0, tiled=True)
    table = half_table(modes_here * peers)
    return synthesis(block, table, STEPS)


def solution(mesh):
    placed = (P("mode", None, "tile"), P("mode", None, None), P("tile", None), P())
    return jax.shard_map(
        shards, mesh=mesh, in_specs=placed, out_specs=P("mode", "tile", None), check_vma=False
    )
```

```python
import math

import jax
import jax.numpy as jnp
import ml_dtypes
import numpy as np
from jax import lax
from jax.experimental import pallas as pl
from jax.experimental.pallas import tpu as pltpu
from jax.sharding import PartitionSpec as P

BF16 = jnp.bfloat16
F32 = jnp.float32
LANES = 128
SUBS = 8
ROWS16 = 16
MIB = 2**20
PIECES = 4
STEPS = (2,) * 8


def row_order(modes):
    return np.concatenate([np.arange(0, modes, 4), np.arange(2, modes, 4), np.arange(1, modes, 2)])


def wave_table(modes, peers):
    angles = 2 * modes
    here = modes // peers
    local = row_order(here)
    cuts = [local[: here // 4], local[here // 4 : here // 2], local[here // 2 :]]
    order = np.concatenate([(np.arange(peers)[:, None] * here + cut).reshape(-1) for cut in cuts])
    order = np.repeat(order, 2)
    phase = (order[:, None] * np.arange(modes)[None, :] % angles).astype(np.float32)
    phase = phase * np.float32(2.0 * math.pi / angles)
    weight = np.where(order == 0, 1.0, 2.0).astype(np.float32) / np.float32(math.sqrt(2.0 * modes))
    part = np.arange(2 * modes) % 2
    wave = np.where((part == 0)[:, None], np.cos(phase), -np.sin(phase)).astype(np.float32)
    return jnp.asarray((weight[:, None] * wave).astype(ml_dtypes.bfloat16))


def one_hot_order(index, owner, hot):
    width = hot.shape[0]
    index = index - owner * width
    spot = lax.broadcasted_iota(jnp.int32, (SUBS, LANES), 0)
    for q in range(SUBS):
        low = index[q : q + 1, :] - spot
        for first in range(0, width, ROWS16):
            pair = [jnp.where(low == first + shift, 1.0, 0.0) for shift in (0, SUBS)]
            hot[first : first + ROWS16, q * LANES : (q + 1) * LANES] = jnp.concatenate(pair, axis=0).astype(BF16)


def box_rows(charges, hot, rows):
    modes, parts, width = charges.shape
    count = modes * parts
    moved = jnp.dot(charges[...].reshape(count, width), hot[...], preferred_element_type=F32)
    for q in range(SUBS):
        rows[pl.ds(q, count, stride=SUBS), :] = moved[:, q * LANES : (q + 1) * LANES]
    return rows[...].astype(BF16)


def owners():
    tile = lax.axis_index("tile")
    toward = 1 - 2 * lax.rem(tile, 2)
    return tile + toward, tile, tile - toward


def lane_slot(o, u, groups):
    return (u + groups // 2) % groups if o == 1 else u


def prepare_kernel(
    boxes,
    charges_hbm,
    skel_hbm,
    lists_hbm,
    proxy_hbm,
    order_ref,
    own_ref,
    pick_ref,
    proxy_ref,
    charges,
    skel,
    lists,
    hot,
    rows,
    sems,
):
    slots = skel.shape[1]
    count, tiles = lists.shape
    cols = count * tiles
    groups = LANES // boxes
    total = skel_hbm.shape[1] // boxes
    places = [jnp.clip(owner, 0, total - 1) for owner in owners()]
    copies = []
    for o, place in enumerate(places):
        column = pl.multiple_of(place // groups * LANES, LANES)
        copies.append(pltpu.make_async_copy(skel_hbm.at[:, pl.ds(column, LANES)], skel.at[o], sems.at[o]))
    copies.append(pltpu.make_async_copy(charges_hbm, charges, sems.at[3]))
    copies.append(pltpu.make_async_copy(lists_hbm, lists, sems.at[4]))
    for copy in copies:
        copy.start()
    modes = proxy_hbm.shape[0]
    per = modes // PIECES
    fetches = []
    for k in range(PIECES):
        span = pl.ds(k * per, per)
        fetches.append(pltpu.make_async_copy(proxy_hbm.at[span], proxy_ref.at[span], sems.at[5 + k]))
        fetches[-1].start()
    pick_ref[...] = jnp.zeros_like(pick_ref)
    for copy in copies:
        copy.wait()
    lane = lax.broadcasted_iota(jnp.int32, (SUBS, LANES), 1)
    for o in (1, 0, 2):
        index = jnp.zeros((SUBS, LANES), jnp.int32)
        for u in range(slots // SUBS):
            v = lane_slot(o, u, groups)
            shift = lax.rem(v * boxes - lax.rem(places[o], groups) * boxes + LANES, LANES)
            moved = pltpu.roll(skel[o, u * SUBS : (u + 1) * SUBS, :], shift, 1)
            index = jnp.where(lane // boxes == v, moved, index)
        one_hot_order(index, places[o], hot if o == 1 else order_ref.at[o // 2])
        if o == 1:
            own_ref[...] = box_rows(charges, hot, rows)
    box = lax.broadcasted_iota(jnp.int32, (boxes, tiles), 0)
    for o, owner in enumerate(owners()):
        for l in range(count):
            block = jnp.where(box == lists[l : l + 1, :] - owner * boxes, 1.0, 0.0).astype(BF16)
            for u in range(groups):
                first = o // 2 * LANES + lane_slot(o, u, groups) * boxes
                pick_ref[first : first + boxes, u * cols + l * tiles : u * cols + (l + 1) * tiles] = block
    for fetch in fetches:
        fetch.wait()


def prepare(charges, skel_t, lists, proxy):
    modes, parts, width = charges.shape
    slots = skel_t.shape[0]
    boxes = width // slots
    count, tiles = lists.shape
    rows = modes * parts * SUBS

    def body(*refs):
        prepare_kernel(boxes, *refs)

    held = pl.BlockSpec(memory_space=pltpu.VMEM)
    return pl.pallas_call(
        body,
        out_shape=[
            pltpu.VMEM((2, width, width), BF16),
            pltpu.VMEM((rows, LANES), BF16),
            pltpu.VMEM((2 * LANES, LANES // boxes * count * tiles), BF16),
            pltpu.VMEM(proxy.shape, BF16),
        ],
        in_specs=[pl.BlockSpec(memory_space=pltpu.HBM)] * 4,
        out_specs=[held] * 4,
        scratch_shapes=[
            pltpu.VMEM(charges.shape, BF16),
            pltpu.VMEM((3, slots, LANES), jnp.int32),
            pltpu.VMEM((count, tiles), jnp.int32),
            pltpu.VMEM((width, width), BF16),
            pltpu.VMEM((rows, LANES), F32),
            pltpu.SemaphoreType.DMA((5 + PIECES,)),
        ],
        compiler_params=pltpu.CompilerParams(vmem_limit_bytes=24 * MIB),
    )(*(pltpu.with_memory_space_constraint(x, pltpu.HBM) for x in (charges, skel_t, lists, proxy)))


def near_rows_kernel(near, order, out, rows):
    out[...] = box_rows(near, order.at[0], rows)


def near_rows(near, order, like):
    held = pl.BlockSpec(memory_space=pltpu.VMEM)
    return pl.pallas_call(
        near_rows_kernel,
        out_shape=pltpu.VMEM(like.shape, BF16),
        in_specs=[held] * 2,
        out_specs=held,
        scratch_shapes=[pltpu.VMEM(like.shape, F32)],
        compiler_params=pltpu.CompilerParams(vmem_limit_bytes=16 * MIB),
    )(near, order)


def field_kernel(groups, tiles, near, own, far, order, pick, proxy, field, picked, rows):
    modes, targets, depth = proxy.shape
    cols = pick.shape[1] // groups
    count = cols // tiles
    first_rows = near[...]
    last_rows = box_rows(far, order.at[1], rows)
    own_rows = own[...]
    low_half = lax.broadcasted_iota(jnp.int32, own_rows.shape, 1) < LANES // 2
    for h in range(groups // 2):
        mixed = jnp.where(low_half, first_rows, own_rows) if h == 0 else jnp.where(low_half, own_rows, first_rows)
        source = jnp.concatenate([mixed, last_rows], axis=1)
        got = jnp.dot(source, pick[:, 2 * h * cols : 2 * (h + 1) * cols], preferred_element_type=F32)
        got = got.reshape(modes, 2, SUBS, 2 * cols)
        for l in range(count):
            low = got[..., l * tiles : (l + 1) * tiles]
            high = got[..., cols + l * tiles : cols + (l + 1) * tiles]
            both = jnp.concatenate([low, high], axis=2).astype(BF16)
            first = l * (groups * SUBS) + h * 2 * SUBS
            for c in range(2):
                picked[:, first : first + 2 * SUBS, c * tiles : (c + 1) * tiles] = both[:, c]
    per = ROWS16 // 2
    local = row_order(modes)
    for g in range(modes // per):
        parts = []
        for j in range(per):
            m = int(local[g * per + j])
            res = jnp.dot(proxy[m], picked[m], preferred_element_type=F32).astype(BF16)
            parts += [res[:, :tiles], res[:, tiles:]]
        span = slice(g * ROWS16, (g + 1) * ROWS16)
        wide = targets // PIECES
        for k in range(PIECES):
            chunk = slice(k * wide, (k + 1) * wide)
            stack = jnp.stack([part[chunk] for part in parts], axis=0)
            field[chunk, span, :] = jnp.swapaxes(stack, 0, 1)


def fields(near, own, far, order, pick, proxy, boxes, tiles):
    modes, targets, depth = proxy.shape
    groups = LANES // boxes

    def body(*refs):
        field_kernel(groups, tiles, *refs)

    held = pl.BlockSpec(memory_space=pltpu.VMEM)
    shape = (targets, 2 * modes, tiles)
    return pl.pallas_call(
        body,
        out_shape=pltpu.VMEM(shape, BF16),
        in_specs=[held] * 6,
        out_specs=held,
        scratch_shapes=[
            pltpu.VMEM((modes, depth, 2 * tiles), BF16),
            pltpu.VMEM(own.shape, F32),
        ],
        compiler_params=pltpu.CompilerParams(vmem_limit_bytes=32 * MIB),
    )(near, own, far, order, pick, proxy)


def synth_kernel(spans, block, table, out_hbm, out, sems):
    peers, targets, rows, tiles = block.shape
    width = table.shape[1]
    quarter = width // 2
    cuts = ((0, rows // 4, quarter), (rows // 4, rows // 2, quarter), (rows // 2, rows, width))
    writes = []
    for k, (lo, hi) in enumerate(spans):
        sums = []
        for first, last, columns in cuts:
            depth = peers * (last - first)
            parts = [block[:, p, first:last, :].reshape(depth, tiles) for p in range(lo, hi)]
            weights = table[peers * first : peers * last, :columns]
            sums.append(
                lax.dot_general(
                    jnp.concatenate(parts, axis=1), weights, (((0,), (0,)), ((), ())), preferred_element_type=F32
                )
            )
        fours, twos, odd = sums
        for s, even in enumerate((fours + twos, fours - twos)):
            near = odd[:, s * quarter : (s + 1) * quarter]
            at = slice(s * quarter, (s + 1) * quarter)
            out[lo:hi, :, at] = (even + near).astype(BF16).reshape(hi - lo, tiles, quarter)
            at = slice(width + s * quarter, width + (s + 1) * quarter)
            out[lo:hi, :, at] = (even - near).astype(BF16).reshape(hi - lo, tiles, quarter)
        writes.append(pltpu.make_async_copy(out.at[lo:hi], out_hbm.at[lo:hi], sems.at[k]))
        writes[-1].start()
    for copy in writes:
        copy.wait()


def synthesis(block, table, steps):
    peers, targets, rows, tiles = block.shape
    angles = 2 * table.shape[1]
    shape = (targets, tiles, angles)
    ends = [sum(steps[: k + 1]) for k in range(len(steps))]
    spans = list(zip([0] + ends[:-1], ends))

    def body(*refs):
        synth_kernel(spans, *refs)

    placed = pl.BlockSpec(memory_space=pltpu.HBM)
    return pl.pallas_call(
        body,
        out_shape=pltpu.HBM(shape, BF16),
        in_specs=[pl.BlockSpec(memory_space=pltpu.VMEM)] * 2,
        out_specs=placed,
        scratch_shapes=[
            pltpu.VMEM(shape, BF16),
            pltpu.SemaphoreType.DMA((len(spans),)),
        ],
        compiler_params=pltpu.CompilerParams(vmem_limit_bytes=16 * MIB),
        cost_estimate=pl.CostEstimate(flops=2**32, bytes_accessed=2**24, transcendentals=0),
    )(pltpu.with_memory_space_constraint(block, pltpu.VMEM), table)


def shards(charges, proxy, tile_boxes, box_skel):
    modes_here, parts, skel_here = charges.shape
    _, targets, _ = proxy.shape
    tiles_here, _ = tile_boxes.shape
    slots = box_skel.shape[1]
    peers = lax.axis_size("mode")
    groups = lax.axis_size("tile")
    far = lax.ppermute(charges, "tile", [(i, i - 1 + 2 * (i % 2)) for i in range(1, groups - 1)])
    near = lax.ppermute(charges, "tile", [(i, i + 1 - 2 * (i % 2)) for i in range(groups)])
    order, own, pick, proxy = prepare(charges, box_skel.T, tile_boxes.T, proxy)
    field = fields(near_rows(near, order, own), own, far, order, pick, proxy, skel_here // slots, tiles_here)
    field = field.reshape(peers, targets // peers, modes_here * parts, tiles_here)
    block = lax.all_to_all(field, "mode", split_axis=0, concat_axis=0, tiled=True)
    table = wave_table(modes_here * peers, peers)
    return synthesis(block, table, STEPS)


def solution(mesh):
    placed = (P("mode", None, "tile"), P("mode", None, None), P("tile", None), P())
    return jax.shard_map(
        shards, mesh=mesh, in_specs=placed, out_specs=P("mode", "tile", None), check_vma=False
    )
```

```python
import math

import jax
import jax.numpy as jnp
import ml_dtypes
import numpy as np
from jax import lax
from jax.experimental import pallas as pl
from jax.experimental.pallas import tpu as pltpu
from jax.sharding import PartitionSpec as P

BF16 = jnp.bfloat16
F32 = jnp.float32
LANES = 128
SUBS = 8
ROWS16 = 16
MIB = 2**20
PIECES = 4
STEPS = (2,) * 8


def row_order(modes):
    return np.concatenate([np.arange(0, modes, 4), np.arange(2, modes, 4), np.arange(1, modes, 2)])


def wave_table(modes, peers):
    angles = 2 * modes
    here = modes // peers
    local = row_order(here)
    cuts = [local[: here // 4], local[here // 4 : here // 2], local[here // 2 :]]
    order = np.concatenate([(np.arange(peers)[:, None] * here + cut).reshape(-1) for cut in cuts])
    order = np.repeat(order, 2)
    phase = (order[:, None] * np.arange(modes)[None, :] % angles).astype(np.float32)
    phase = phase * np.float32(2.0 * math.pi / angles)
    weight = np.where(order == 0, 1.0, 2.0).astype(np.float32) / np.float32(math.sqrt(2.0 * modes))
    part = np.arange(2 * modes) % 2
    wave = np.where((part == 0)[:, None], np.cos(phase), -np.sin(phase)).astype(np.float32)
    return jnp.asarray((weight[:, None] * wave).astype(ml_dtypes.bfloat16))


def one_hot_order(index, owner, hot):
    width = hot.shape[0]
    index = index - owner * width
    spot = lax.broadcasted_iota(jnp.int32, (SUBS, LANES), 0)
    for q in range(SUBS):
        low = index[q : q + 1, :] - spot
        for first in range(0, width, ROWS16):
            pair = [jnp.where(low == first + shift, 1.0, 0.0) for shift in (0, SUBS)]
            hot[first : first + ROWS16, q * LANES : (q + 1) * LANES] = jnp.concatenate(pair, axis=0).astype(BF16)


def box_rows(charges, hot, rows):
    modes, parts, width = charges.shape
    count = modes * parts
    moved = jnp.dot(charges[...].reshape(count, width), hot[...], preferred_element_type=F32)
    for q in range(SUBS):
        rows[pl.ds(q, count, stride=SUBS), :] = moved[:, q * LANES : (q + 1) * LANES]
    return rows[...].astype(BF16)


def owners():
    tile = lax.axis_index("tile")
    toward = 1 - 2 * lax.rem(tile, 2)
    return tile + toward, tile, tile - toward


def lane_slot(o, u, groups):
    return (u + groups // 2) % groups if o == 1 else u


def prepare_kernel(
    boxes,
    charges_hbm,
    skel_hbm,
    lists_hbm,
    proxy_hbm,
    order_ref,
    own_ref,
    pick_ref,
    proxy_ref,
    charges,
    skel,
    lists,
    hot,
    rows,
    sems,
):
    slots = skel.shape[1]
    count, tiles = lists.shape
    cols = count * tiles
    groups = LANES // boxes
    total = skel_hbm.shape[1] // boxes
    places = [jnp.clip(owner, 0, total - 1) for owner in owners()]
    copies = []
    for o, place in enumerate(places):
        column = pl.multiple_of(place // groups * LANES, LANES)
        copies.append(pltpu.make_async_copy(skel_hbm.at[:, pl.ds(column, LANES)], skel.at[o], sems.at[o]))
    copies.append(pltpu.make_async_copy(charges_hbm, charges, sems.at[3]))
    copies.append(pltpu.make_async_copy(lists_hbm, lists, sems.at[4]))
    for copy in copies:
        copy.start()
    modes = proxy_hbm.shape[0]
    per = modes // PIECES
    fetches = []
    for k in range(PIECES):
        span = pl.ds(k * per, per)
        fetches.append(pltpu.make_async_copy(proxy_hbm.at[span], proxy_ref.at[span], sems.at[5 + k]))
        fetches[-1].start()
    pick_ref[...] = jnp.zeros_like(pick_ref)
    for copy in copies:
        copy.wait()
    lane = lax.broadcasted_iota(jnp.int32, (SUBS, LANES), 1)
    for o in (1, 0, 2):
        index = jnp.zeros((SUBS, LANES), jnp.int32)
        for u in range(slots // SUBS):
            v = lane_slot(o, u, groups)
            shift = lax.rem(v * boxes - lax.rem(places[o], groups) * boxes + LANES, LANES)
            moved = pltpu.roll(skel[o, u * SUBS : (u + 1) * SUBS, :], shift, 1)
            index = jnp.where(lane // boxes == v, moved, index)
        one_hot_order(index, places[o], hot if o == 1 else order_ref.at[o // 2])
        if o == 1:
            own_ref[...] = box_rows(charges, hot, rows)
    box = lax.broadcasted_iota(jnp.int32, (boxes, tiles), 0)
    for o, owner in enumerate(owners()):
        for l in range(count):
            block = jnp.where(box == lists[l : l + 1, :] - owner * boxes, 1.0, 0.0).astype(BF16)
            for u in range(groups):
                first = o // 2 * LANES + lane_slot(o, u, groups) * boxes
                pick_ref[first : first + boxes, u * cols + l * tiles : u * cols + (l + 1) * tiles] = block
    for fetch in fetches:
        fetch.wait()


def prepare(charges, skel_t, lists, proxy):
    modes, parts, width = charges.shape
    slots = skel_t.shape[0]
    boxes = width // slots
    count, tiles = lists.shape
    rows = modes * parts * SUBS

    def body(*refs):
        prepare_kernel(boxes, *refs)

    held = pl.BlockSpec(memory_space=pltpu.VMEM)
    return pl.pallas_call(
        body,
        out_shape=[
            pltpu.VMEM((2, width, width), BF16),
            pltpu.VMEM((rows, LANES), BF16),
            pltpu.VMEM((2 * LANES, LANES // boxes * count * tiles), BF16),
            pltpu.VMEM(proxy.shape, BF16),
        ],
        in_specs=[pl.BlockSpec(memory_space=pltpu.HBM)] * 4,
        out_specs=[held] * 4,
        scratch_shapes=[
            pltpu.VMEM(charges.shape, BF16),
            pltpu.VMEM((3, slots, LANES), jnp.int32),
            pltpu.VMEM((count, tiles), jnp.int32),
            pltpu.VMEM((width, width), BF16),
            pltpu.VMEM((rows, LANES), F32),
            pltpu.SemaphoreType.DMA((5 + PIECES,)),
        ],
        compiler_params=pltpu.CompilerParams(vmem_limit_bytes=24 * MIB),
    )(*(pltpu.with_memory_space_constraint(x, pltpu.HBM) for x in (charges, skel_t, lists, proxy)))


def far_rows_kernel(far, order, out, rows):
    out[...] = box_rows(far, order.at[1], rows)


def far_rows(far, order, like):
    held = pl.BlockSpec(memory_space=pltpu.VMEM)
    return pl.pallas_call(
        far_rows_kernel,
        out_shape=pltpu.VMEM(like.shape, BF16),
        in_specs=[held] * 2,
        out_specs=held,
        scratch_shapes=[pltpu.VMEM(like.shape, F32)],
        compiler_params=pltpu.CompilerParams(vmem_limit_bytes=16 * MIB),
    )(far, order)


def field_kernel(groups, tiles, far, own, near, order, pick, proxy, field, picked, rows):
    modes, targets, depth = proxy.shape
    cols = pick.shape[1] // groups
    count = cols // tiles
    first_rows = box_rows(near, order.at[0], rows)
    last_rows = far[...]
    own_rows = own[...]
    low_half = lax.broadcasted_iota(jnp.int32, own_rows.shape, 1) < LANES // 2
    for h in range(groups // 2):
        mixed = jnp.where(low_half, first_rows, own_rows) if h == 0 else jnp.where(low_half, own_rows, first_rows)
        source = jnp.concatenate([mixed, last_rows], axis=1)
        got = jnp.dot(source, pick[:, 2 * h * cols : 2 * (h + 1) * cols], preferred_element_type=F32)
        got = got.reshape(modes, 2, SUBS, 2 * cols)
        for l in range(count):
            low = got[..., l * tiles : (l + 1) * tiles]
            high = got[..., cols + l * tiles : cols + (l + 1) * tiles]
            both = jnp.concatenate([low, high], axis=2).astype(BF16)
            first = l * (groups * SUBS) + h * 2 * SUBS
            for c in range(2):
                picked[:, first : first + 2 * SUBS, c * tiles : (c + 1) * tiles] = both[:, c]
    per = ROWS16 // 2
    local = row_order(modes)
    for g in range(modes // per):
        parts = []
        for j in range(per):
            m = int(local[g * per + j])
            res = jnp.dot(proxy[m], picked[m], preferred_element_type=F32).astype(BF16)
            parts += [res[:, :tiles], res[:, tiles:]]
        span = slice(g * ROWS16, (g + 1) * ROWS16)
        wide = targets // PIECES
        for k in range(PIECES):
            chunk = slice(k * wide, (k + 1) * wide)
            stack = jnp.stack([part[chunk] for part in parts], axis=0)
            field[chunk, span, :] = jnp.swapaxes(stack, 0, 1)


def fields(far, own, near, order, pick, proxy, boxes, tiles):
    modes, targets, depth = proxy.shape
    groups = LANES // boxes

    def body(*refs):
        field_kernel(groups, tiles, *refs)

    held = pl.BlockSpec(memory_space=pltpu.VMEM)
    shape = (targets, 2 * modes, tiles)
    return pl.pallas_call(
        body,
        out_shape=pltpu.VMEM(shape, BF16),
        in_specs=[held] * 6,
        out_specs=held,
        scratch_shapes=[
            pltpu.VMEM((modes, depth, 2 * tiles), BF16),
            pltpu.VMEM(own.shape, F32),
        ],
        compiler_params=pltpu.CompilerParams(vmem_limit_bytes=32 * MIB),
    )(far, own, near, order, pick, proxy)


def synth_kernel(spans, block, table, out_hbm, out, sems):
    peers, targets, rows, tiles = block.shape
    width = table.shape[1]
    quarter = width // 2
    cuts = ((0, rows // 4, quarter), (rows // 4, rows // 2, quarter), (rows // 2, rows, width))
    writes = []
    for k, (lo, hi) in enumerate(spans):
        sums = []
        for first, last, columns in cuts:
            depth = peers * (last - first)
            parts = [block[:, p, first:last, :].reshape(depth, tiles) for p in range(lo, hi)]
            weights = table[peers * first : peers * last, :columns]
            sums.append(
                lax.dot_general(
                    jnp.concatenate(parts, axis=1), weights, (((0,), (0,)), ((), ())), preferred_element_type=F32
                )
            )
        fours, twos, odd = sums
        for s, even in enumerate((fours + twos, fours - twos)):
            near = odd[:, s * quarter : (s + 1) * quarter]
            at = slice(s * quarter, (s + 1) * quarter)
            out[lo:hi, :, at] = (even + near).astype(BF16).reshape(hi - lo, tiles, quarter)
            at = slice(width + s * quarter, width + (s + 1) * quarter)
            out[lo:hi, :, at] = (even - near).astype(BF16).reshape(hi - lo, tiles, quarter)
        writes.append(pltpu.make_async_copy(out.at[lo:hi], out_hbm.at[lo:hi], sems.at[k]))
        writes[-1].start()
    for copy in writes:
        copy.wait()


def synthesis(block, table, steps):
    peers, targets, rows, tiles = block.shape
    angles = 2 * table.shape[1]
    shape = (targets, tiles, angles)
    ends = [sum(steps[: k + 1]) for k in range(len(steps))]
    spans = list(zip([0] + ends[:-1], ends))

    def body(*refs):
        synth_kernel(spans, *refs)

    placed = pl.BlockSpec(memory_space=pltpu.HBM)
    return pl.pallas_call(
        body,
        out_shape=pltpu.HBM(shape, BF16),
        in_specs=[pl.BlockSpec(memory_space=pltpu.VMEM)] * 2,
        out_specs=placed,
        scratch_shapes=[
            pltpu.VMEM(shape, BF16),
            pltpu.SemaphoreType.DMA((len(spans),)),
        ],
        compiler_params=pltpu.CompilerParams(vmem_limit_bytes=16 * MIB),
        cost_estimate=pl.CostEstimate(flops=2**32, bytes_accessed=2**24, transcendentals=0),
    )(pltpu.with_memory_space_constraint(block, pltpu.VMEM), table)


def shards(charges, proxy, tile_boxes, box_skel):
    modes_here, parts, skel_here = charges.shape
    _, targets, _ = proxy.shape
    tiles_here, _ = tile_boxes.shape
    slots = box_skel.shape[1]
    peers = lax.axis_size("mode")
    groups = lax.axis_size("tile")
    far = lax.ppermute(charges, "tile", [(i, i - 1 + 2 * (i % 2)) for i in range(1, groups - 1)])
    near = lax.ppermute(charges, "tile", [(i, i + 1 - 2 * (i % 2)) for i in range(groups)])
    order, own, pick, proxy = prepare(charges, box_skel.T, tile_boxes.T, proxy)
    field = fields(far_rows(far, order, own), own, near, order, pick, proxy, skel_here // slots, tiles_here)
    field = field.reshape(peers, targets // peers, modes_here * parts, tiles_here)
    block = lax.all_to_all(field, "mode", split_axis=0, concat_axis=0, tiled=True)
    table = wave_table(modes_here * peers, peers)
    return synthesis(block, table, STEPS)


def solution(mesh):
    placed = (P("mode", None, "tile"), P("mode", None, None), P("tile", None), P())
    return jax.shard_map(
        shards, mesh=mesh, in_specs=placed, out_specs=P("mode", "tile", None), check_vma=False
    )
```

```python
import math

import jax
import jax.numpy as jnp
import ml_dtypes
import numpy as np
from jax import lax
from jax.experimental import pallas as pl
from jax.experimental.pallas import tpu as pltpu
from jax.sharding import PartitionSpec as P

BF16 = jnp.bfloat16
F32 = jnp.float32
LANES = 128
SUBS = 8
ROWS16 = 16
MIB = 2**20
PIECES = 4
STEPS = (2,) * 8


def row_order(modes):
    return np.concatenate([np.arange(0, modes, 4), np.arange(2, modes, 4), np.arange(1, modes, 2)])


def wave_table(modes, peers):
    angles = 2 * modes
    here = modes // peers
    local = row_order(here)
    cuts = [local[: here // 4], local[here // 4 : here // 2], local[here // 2 :]]
    order = np.concatenate([(np.arange(peers)[:, None] * here + cut).reshape(-1) for cut in cuts])
    order = np.repeat(order, 2)
    phase = (order[:, None] * np.arange(modes)[None, :] % angles).astype(np.float32)
    phase = phase * np.float32(2.0 * math.pi / angles)
    weight = np.where(order == 0, 1.0, 2.0).astype(np.float32) / np.float32(math.sqrt(2.0 * modes))
    part = np.arange(2 * modes) % 2
    wave = np.where((part == 0)[:, None], np.cos(phase), -np.sin(phase)).astype(np.float32)
    return jnp.asarray((weight[:, None] * wave).astype(ml_dtypes.bfloat16))


def one_hot_order(index, owner, hot):
    width = hot.shape[0]
    index = index - owner * width
    spot = lax.broadcasted_iota(jnp.int32, (SUBS, LANES), 0)
    for q in range(SUBS):
        low = index[q : q + 1, :] - spot
        for first in range(0, width, ROWS16):
            pair = [jnp.where(low == first + shift, 1.0, 0.0) for shift in (0, SUBS)]
            hot[first : first + ROWS16, q * LANES : (q + 1) * LANES] = jnp.concatenate(pair, axis=0).astype(BF16)


def box_rows(charges, hot, rows):
    modes, parts, width = charges.shape
    count = modes * parts
    moved = jnp.dot(charges[...].reshape(count, width), hot[...], preferred_element_type=F32)
    for q in range(SUBS):
        rows[pl.ds(q, count, stride=SUBS), :] = moved[:, q * LANES : (q + 1) * LANES]
    return rows[...].astype(BF16)


def owners():
    tile = lax.axis_index("tile")
    toward = 1 - 2 * lax.rem(tile, 2)
    return tile + toward, tile, tile - toward


def lane_slot(o, u, groups):
    return (u + groups // 2) % groups if o == 1 else u


def prepare_kernel(
    boxes,
    charges_hbm,
    skel_hbm,
    lists_hbm,
    proxy_hbm,
    order_ref,
    own_ref,
    pick_ref,
    proxy_ref,
    charges,
    skel,
    lists,
    hot,
    rows,
    sems,
):
    slots = skel.shape[1]
    count, tiles = lists.shape
    cols = count * tiles
    groups = LANES // boxes
    total = skel_hbm.shape[1] // boxes
    places = [jnp.clip(owner, 0, total - 1) for owner in owners()]
    copies = []
    for o, place in enumerate(places):
        column = pl.multiple_of(place // groups * LANES, LANES)
        copies.append(pltpu.make_async_copy(skel_hbm.at[:, pl.ds(column, LANES)], skel.at[o], sems.at[o]))
    copies.append(pltpu.make_async_copy(charges_hbm, charges, sems.at[3]))
    copies.append(pltpu.make_async_copy(lists_hbm, lists, sems.at[4]))
    for copy in copies:
        copy.start()
    modes = proxy_hbm.shape[0]
    per = modes // PIECES
    fetches = []
    for k in range(PIECES):
        span = pl.ds(k * per, per)
        fetches.append(pltpu.make_async_copy(proxy_hbm.at[span], proxy_ref.at[span], sems.at[5 + k]))
        fetches[-1].start()
    pick_ref[...] = jnp.zeros_like(pick_ref)
    for copy in copies:
        copy.wait()
    lane = lax.broadcasted_iota(jnp.int32, (SUBS, LANES), 1)
    for o in (1, 0, 2):
        index = jnp.zeros((SUBS, LANES), jnp.int32)
        for u in range(slots // SUBS):
            v = lane_slot(o, u, groups)
            shift = lax.rem(v * boxes - lax.rem(places[o], groups) * boxes + LANES, LANES)
            moved = pltpu.roll(skel[o, u * SUBS : (u + 1) * SUBS, :], shift, 1)
            index = jnp.where(lane // boxes == v, moved, index)
        one_hot_order(index, places[o], hot if o == 1 else order_ref.at[o // 2])
        if o == 1:
            own_ref[...] = box_rows(charges, hot, rows)
    box = lax.broadcasted_iota(jnp.int32, (boxes, tiles), 0)
    for o, owner in enumerate(owners()):
        for l in range(count):
            block = jnp.where(box == lists[l : l + 1, :] - owner * boxes, 1.0, 0.0).astype(BF16)
            for u in range(groups):
                first = o // 2 * LANES + lane_slot(o, u, groups) * boxes
                pick_ref[first : first + boxes, u * cols + l * tiles : u * cols + (l + 1) * tiles] = block
    for fetch in fetches:
        fetch.wait()


def prepare(charges, skel_t, lists, proxy):
    modes, parts, width = charges.shape
    slots = skel_t.shape[0]
    boxes = width // slots
    count, tiles = lists.shape
    rows = modes * parts * SUBS

    def body(*refs):
        prepare_kernel(boxes, *refs)

    held = pl.BlockSpec(memory_space=pltpu.VMEM)
    return pl.pallas_call(
        body,
        out_shape=[
            pltpu.VMEM((2, width, width), BF16),
            pltpu.VMEM((rows, LANES), BF16),
            pltpu.VMEM((2 * LANES, LANES // boxes * count * tiles), BF16),
            pltpu.VMEM(proxy.shape, BF16),
        ],
        in_specs=[pl.BlockSpec(memory_space=pltpu.HBM)] * 4,
        out_specs=[held] * 4,
        scratch_shapes=[
            pltpu.VMEM(charges.shape, BF16),
            pltpu.VMEM((3, slots, LANES), jnp.int32),
            pltpu.VMEM((count, tiles), jnp.int32),
            pltpu.VMEM((width, width), BF16),
            pltpu.VMEM((rows, LANES), F32),
            pltpu.SemaphoreType.DMA((5 + PIECES,)),
        ],
        compiler_params=pltpu.CompilerParams(vmem_limit_bytes=24 * MIB),
    )(*(pltpu.with_memory_space_constraint(x, pltpu.HBM) for x in (charges, skel_t, lists, proxy)))


def near_rows_kernel(near, order, own, out, rows):
    first_rows = box_rows(near, order.at[0], rows)
    own_rows = own[...]
    low_half = lax.broadcasted_iota(jnp.int32, own_rows.shape, 1) < LANES // 2
    out[0] = jnp.where(low_half, first_rows, own_rows)
    out[1] = jnp.where(low_half, own_rows, first_rows)


def near_rows(near, order, own):
    held = pl.BlockSpec(memory_space=pltpu.VMEM)
    return pl.pallas_call(
        near_rows_kernel,
        out_shape=pltpu.VMEM((2,) + own.shape, BF16),
        in_specs=[held] * 3,
        out_specs=held,
        scratch_shapes=[pltpu.VMEM(own.shape, F32)],
        compiler_params=pltpu.CompilerParams(vmem_limit_bytes=16 * MIB),
    )(near, order, own)


def field_kernel(groups, tiles, mixed, far, order, pick, proxy, field, picked, rows):
    modes, targets, depth = proxy.shape
    cols = pick.shape[1] // groups
    count = cols // tiles
    last_rows = box_rows(far, order.at[1], rows)
    for h in range(groups // 2):
        source = jnp.concatenate([mixed[h], last_rows], axis=1)
        got = jnp.dot(source, pick[:, 2 * h * cols : 2 * (h + 1) * cols], preferred_element_type=F32)
        got = got.reshape(modes, 2, SUBS, 2 * cols)
        for l in range(count):
            low = got[..., l * tiles : (l + 1) * tiles]
            high = got[..., cols + l * tiles : cols + (l + 1) * tiles]
            both = jnp.concatenate([low, high], axis=2).astype(BF16)
            first = l * (groups * SUBS) + h * 2 * SUBS
            for c in range(2):
                picked[:, first : first + 2 * SUBS, c * tiles : (c + 1) * tiles] = both[:, c]
    per = ROWS16 // 2
    local = row_order(modes)
    for g in range(modes // per):
        parts = []
        for j in range(per):
            m = int(local[g * per + j])
            res = jnp.dot(proxy[m], picked[m], preferred_element_type=F32).astype(BF16)
            parts += [res[:, :tiles], res[:, tiles:]]
        span = slice(g * ROWS16, (g + 1) * ROWS16)
        wide = targets // PIECES
        for k in range(PIECES):
            chunk = slice(k * wide, (k + 1) * wide)
            stack = jnp.stack([part[chunk] for part in parts], axis=0)
            field[chunk, span, :] = jnp.swapaxes(stack, 0, 1)


def fields(mixed, far, order, pick, proxy, boxes, tiles):
    modes, targets, depth = proxy.shape
    groups = LANES // boxes

    def body(*refs):
        field_kernel(groups, tiles, *refs)

    held = pl.BlockSpec(memory_space=pltpu.VMEM)
    shape = (targets, 2 * modes, tiles)
    return pl.pallas_call(
        body,
        out_shape=pltpu.VMEM(shape, BF16),
        in_specs=[held] * 5,
        out_specs=held,
        scratch_shapes=[
            pltpu.VMEM((modes, depth, 2 * tiles), BF16),
            pltpu.VMEM(mixed.shape[1:], F32),
        ],
        compiler_params=pltpu.CompilerParams(vmem_limit_bytes=32 * MIB),
    )(mixed, far, order, pick, proxy)


def synth_kernel(spans, block, table, out_hbm, out, sems):
    peers, targets, rows, tiles = block.shape
    width = table.shape[1]
    quarter = width // 2
    cuts = ((0, rows // 4, quarter), (rows // 4, rows // 2, quarter), (rows // 2, rows, width))
    writes = []
    for k, (lo, hi) in enumerate(spans):
        sums = []
        for first, last, columns in cuts:
            depth = peers * (last - first)
            parts = [block[:, p, first:last, :].reshape(depth, tiles) for p in range(lo, hi)]
            weights = table[peers * first : peers * last, :columns]
            sums.append(
                lax.dot_general(
                    jnp.concatenate(parts, axis=1), weights, (((0,), (0,)), ((), ())), preferred_element_type=F32
                )
            )
        fours, twos, odd = sums
        for s, even in enumerate((fours + twos, fours - twos)):
            near = odd[:, s * quarter : (s + 1) * quarter]
            at = slice(s * quarter, (s + 1) * quarter)
            out[lo:hi, :, at] = (even + near).astype(BF16).reshape(hi - lo, tiles, quarter)
            at = slice(width + s * quarter, width + (s + 1) * quarter)
            out[lo:hi, :, at] = (even - near).astype(BF16).reshape(hi - lo, tiles, quarter)
        writes.append(pltpu.make_async_copy(out.at[lo:hi], out_hbm.at[lo:hi], sems.at[k]))
        writes[-1].start()
    for copy in writes:
        copy.wait()


def synthesis(block, table, steps):
    peers, targets, rows, tiles = block.shape
    angles = 2 * table.shape[1]
    shape = (targets, tiles, angles)
    ends = [sum(steps[: k + 1]) for k in range(len(steps))]
    spans = list(zip([0] + ends[:-1], ends))

    def body(*refs):
        synth_kernel(spans, *refs)

    placed = pl.BlockSpec(memory_space=pltpu.HBM)
    return pl.pallas_call(
        body,
        out_shape=pltpu.HBM(shape, BF16),
        in_specs=[pl.BlockSpec(memory_space=pltpu.VMEM)] * 2,
        out_specs=placed,
        scratch_shapes=[
            pltpu.VMEM(shape, BF16),
            pltpu.SemaphoreType.DMA((len(spans),)),
        ],
        compiler_params=pltpu.CompilerParams(vmem_limit_bytes=16 * MIB),
        cost_estimate=pl.CostEstimate(flops=2**32, bytes_accessed=2**24, transcendentals=0),
    )(pltpu.with_memory_space_constraint(block, pltpu.VMEM), table)


def shards(charges, proxy, tile_boxes, box_skel):
    modes_here, parts, skel_here = charges.shape
    _, targets, _ = proxy.shape
    tiles_here, _ = tile_boxes.shape
    slots = box_skel.shape[1]
    peers = lax.axis_size("mode")
    groups = lax.axis_size("tile")
    far = lax.ppermute(charges, "tile", [(i, i - 1 + 2 * (i % 2)) for i in range(1, groups - 1)])
    near = lax.ppermute(charges, "tile", [(i, i + 1 - 2 * (i % 2)) for i in range(groups)])
    order, own, pick, proxy = prepare(charges, box_skel.T, tile_boxes.T, proxy)
    field = fields(near_rows(near, order, own), far, order, pick, proxy, skel_here // slots, tiles_here)
    field = field.reshape(peers, targets // peers, modes_here * parts, tiles_here)
    block = lax.all_to_all(field, "mode", split_axis=0, concat_axis=0, tiled=True)
    table = wave_table(modes_here * peers, peers)
    return synthesis(block, table, STEPS)


def solution(mesh):
    placed = (P("mode", None, "tile"), P("mode", None, None), P("tile", None), P())
    return jax.shard_map(
        shards, mesh=mesh, in_specs=placed, out_specs=P("mode", "tile", None), check_vma=False
    )
```
